512 devices in a mesh: lat: 4 (over x_lo, core), lon: 128 (over z, x_hi, y).
Axes of the slice: x: 4 (x_hi: 2, x_lo: 2; x = x_hi * 2 + x_lo), y: 4, z: 16, core: 2. Of those that a mesh axis runs over, the one named last changes fastest.
Arguments:
- coarse: bfloat16 [16, 4096, 256], P('lat', 'lon'), may hold values from -6 to 6
- w_first: bfloat16 [9, 256, 128], P(None, 'lon'), may hold values from -0.125 to 0.125
- w_second: bfloat16 [9, 128, 128], P(None, 'lon'), may hold values from -0.1875 to 0.1875
- w_skip: bfloat16 [256, 128], P('lon'), may hold values from -0.375 to 0.375
- cotangent: bfloat16 [32, 8192, 128], P('lat', 'lon'), may hold values from -6 to 6
Outputs:
- result: bfloat16 [32, 8192, 128], P('lat', 'lon')
- coarse_gradient: bfloat16 [16, 4096, 256], P('lat', 'lon')
- grad_first: float32 [9, 256, 128], P(None, 'lon')
- grad_second: float32 [9, 128, 128], P(None, 'lon')
- grad_skip: float32 [256, 128], P('lon')
The draws below stay inside these ranges and needn't reach their ends.
All inputs are finite; a program needn't handle non-finite values.
Results may differ from the reference program's by a relative error of at most 0.014.
Values may be sent and summed in bfloat16 or wider, within the bound.
No kernel may reach another device: no remote copies, remote signals or barrier semaphores. Data moves between devices by JAX's collectives and lax.ppermute only.
A program may use at most 64 MiB of HBM per device.

```python
import jax
import jax.numpy as jnp
from jax import lax

C_IN = 256
C_OUT = 128
NR = 32
NC = 8192
MR = 16
MC = 4096


def block_scale(key, extent, cuts, low, largest):
    def one(axis_at, parts):
        steps = jax.random.uniform(jax.random.fold_in(jax.random.fold_in(key, 6), axis_at), (parts,), jnp.float32, low / len(cuts), largest / len(cuts))
        return jnp.repeat(jnp.exp(steps), extent[axis_at] // parts).reshape((-1,) + (1,) * (len(extent) - axis_at - 1))

    loudness = one(*cuts[0])
    for cut in cuts[1:]:
        loudness = loudness * one(*cut)
    return loudness


def gaussian(stream_key, dims, deviation, reach, cuts=(), kind=jnp.bfloat16):
    values = jax.random.normal(stream_key, dims, jnp.float32) * deviation
    if len(cuts) > 0:
        values = block_scale(stream_key, dims, cuts, -0.22, 0.18) * values
    return jnp.clip(values, min=-reach, max=reach).astype(kind)


def setup_inputs(seed: int = 0) -> dict:
    keys = jax.random.split(jax.random.key(seed), 6)
    coarse = gaussian(keys[0], (MR, MC, C_IN), 1.0, 6.0, ((0, 4), (1, 128)))
    w_first = gaussian(keys[1], (9, C_IN, C_OUT), (9 * C_IN) ** -0.5, 0.125, ((1, 128),))
    w_second = gaussian(keys[2], (9, C_OUT, C_OUT), (9 * C_OUT) ** -0.5, 0.1875, ((1, 128),))
    w_skip = gaussian(keys[3], (C_IN, C_OUT), C_IN ** -0.5, 0.375, ((0, 128),))
    cotangent = gaussian(keys[4], (NR, NC, C_OUT), 1.0, 6.0, ((0, 4), (1, 128)))
    return dict(coarse=coarse, w_first=w_first, w_second=w_second, w_skip=w_skip, cotangent=cotangent)


def displace(input_field, offset, along_axis, is_periodic):
    if offset == 0:
        return input_field
    if is_periodic:
        return jnp.roll(input_field, -offset, along_axis)
    length = input_field.shape[along_axis]
    widths = [(0, 0)] * input_field.ndim
    widths[along_axis] = (max(-offset, 0), max(offset, 0))
    padded = jnp.pad(input_field, widths)
    return lax.slice_in_dim(padded, max(offset, 0), max(offset, 0) + length, 1, along_axis)

def upsample_axis(input_field, along_axis, is_periodic):
    before = displace(input_field, -1, along_axis, is_periodic)
    following = displace(input_field, 1, along_axis, is_periodic)
    even_part = 0.75 * input_field + 0.25 * before
    odd_part = 0.75 * input_field + 0.25 * following
    stacked = jnp.stack([even_part, odd_part], along_axis + 1)
    new_shape = list(input_field.shape)
    new_shape[along_axis] = new_shape[along_axis] * 2
    return stacked.reshape(new_shape)

def decimate_axis(input_field, along_axis, is_periodic):
    length = input_field.shape[along_axis] // 2
    split = input_field.reshape(input_field.shape[:along_axis] + (length, 2) + input_field.shape[along_axis + 1:])
    even_part = lax.index_in_dim(split, 0, along_axis + 1, keepdims=False)
    odd_part = lax.index_in_dim(split, 1, along_axis + 1, keepdims=False)
    return 0.75 * (even_part + odd_part) + 0.25 * (displace(odd_part, -1, along_axis, is_periodic) + displace(even_part, 1, along_axis, is_periodic))

def shifted_view(input_field, i, j):
    return displace(displace(input_field, i - 1, 0, False), j - 1, 1, True)

def convolve(input_field, kernels):
    row_count, col_count = (input_field.shape[0], input_field.shape[1])
    summed = None
    for i in range(3):
        for j in range(3):
            window = shifted_view(input_field, i, j).reshape(row_count * col_count, -1)
            partial_value = jnp.dot(window, kernels[3 * i + j], preferred_element_type=jnp.float32)
            summed = partial_value if summed is None else summed + partial_value
    return summed.reshape(row_count, col_count, -1)

def flipped(kernels):
    return jnp.swapaxes(kernels[::-1], 1, 2)

def tap_grads(input_field, cot):
    flat_cot = cot.reshape(-1, cot.shape[-1])
    pieces = []
    for i in range(3):
        for j in range(3):
            window = shifted_view(input_field, i, j).reshape(flat_cot.shape[0], -1)
            pieces.append(lax.dot_general(window, flat_cot, (((0,), (0,)), ((), ())), preferred_element_type=jnp.float32))
    return jnp.stack(pieces, 0)

def reference(coarse, w_first, w_second, w_skip, cotangent):
    wide = coarse.astype(jnp.float32)
    wide = upsample_axis(wide, 0, False)
    wide = upsample_axis(wide, 1, True)
    fine_in = wide.astype(jnp.bfloat16)
    row_count, col_count = (fine_in.shape[0], fine_in.shape[1])
    scale = 1.0 / jnp.sqrt(jnp.float32(row_count * col_count))
    flat_in = fine_in.reshape(row_count * col_count, -1)
    flat_cot = cotangent.reshape(row_count * col_count, -1)
    act = convolve(fine_in, w_first)
    hidden = jax.nn.silu(act).astype(jnp.bfloat16)
    skip_term = jnp.dot(flat_in, w_skip, preferred_element_type=jnp.float32).reshape(row_count, col_count, -1)
    result = (convolve(hidden, w_second) + skip_term).astype(jnp.bfloat16)
    grad_hidden = convolve(cotangent, flipped(w_second))
    sigma = jax.nn.sigmoid(act)
    grad_act = (grad_hidden * sigma * (1.0 + act * (1.0 - sigma))).astype(jnp.bfloat16)
    back_skip = jnp.dot(flat_cot, w_skip.T, preferred_element_type=jnp.float32).reshape(row_count, col_count, -1)
    fine_gradient = (convolve(grad_act, flipped(w_first)) + back_skip).astype(jnp.bfloat16)
    reduced_field = decimate_axis(fine_gradient.astype(jnp.float32), 1, True)
    coarse_gradient = decimate_axis(reduced_field, 0, False).astype(jnp.bfloat16)
    grad_first = tap_grads(fine_in, grad_act) * scale
    grad_second = tap_grads(hidden, cotangent) * scale
    grad_skip = lax.dot_general(flat_in, flat_cot, (((0,), (0,)), ((), ())), preferred_element_type=jnp.float32) * scale
    return (result, coarse_gradient, grad_first, grad_second, grad_skip)
```

```python
import functools

import jax
import jax.numpy as jnp
import numpy as np
from jax import lax
from jax.experimental import pallas as pl
from jax.experimental.pallas import tpu as pltpu
from jax.sharding import Mesh, PartitionSpec as P

PITCH = 80
LENGTH = 14 * PITCH + 16
WIDE = (PITCH, 12 * PITCH + 96)
MIDDLE = (2 * PITCH, 12 * PITCH + 16)
HIDDEN = (2 * PITCH + 16, 12 * PITCH)
INNER = (256, 880)
F32 = jnp.float32
BF16 = jnp.bfloat16
SCALE = 1.0 / 512.0
LAT = ("xl", "core")
LON = ("z", "xh", "y")
PLANE = ("xl", "core", "xh", "y")


def upsampling_matrices():
    taps = {}
    for parity in range(2):
        for dc in (-1, 0, 1):
            for u in range(PITCH):
                row, col = (parity - 1, 64 + u + dc) if u < 8 else (parity, u - 16 + dc)
                if not -3 <= col <= 66:
                    continue
                for wr, m in ((0.75, row // 2), (0.25, row // 2 + (1 if row % 2 else -1))):
                    for wc, n in ((0.75, col // 2), (0.25, col // 2 + (1 if col % 2 else -1))):
                        taps[parity, (dc + 1) * PITCH + u, (m + 1) * 48 + n % 48] = wr * wc
    out = np.zeros((2, 3 * PITCH, 144), np.float32)
    for place, weight in taps.items():
        out[place] = weight
    return out


def decimation_matrix():
    out = np.zeros((32, 4 * PITCH + 16), np.float32)
    weights = (0.25, 0.75, 0.75, 0.25)
    for j in range(32):
        for a in range(4):
            for b in range(4):
                out[j, a * PITCH + 16 + 2 * j - 1 + b] = weights[a] * weights[b]
    return out


def channel_orders():
    spread = np.zeros((256, 256), np.float32)
    pairs = np.zeros((256, 256), np.float32)
    for p in range(8):
        for z in range(16):
            for k in range(2):
                spread[z * 16 + p * 2 + k, p * 32 + z * 2 + k] = 1.0
                pairs[k * 128 + z * 8 + p, p * 32 + z * 2 + k] = 1.0
    return spread, pairs


def dot(a, b):
    return lax.dot_general(a, b, (((1,), (0,)), ((), ())), preferred_element_type=F32)


def dot_nt(a, b):
    return lax.dot_general(a, b, (((1,), (1,)), ((), ())), preferred_element_type=F32)


def inside(bounds_ref, begin, shape):
    place = lax.broadcasted_iota(jnp.int32, shape, 0) + begin
    return (place >= bounds_ref[0]) & (place < bounds_ref[1])


def shifted(field):
    count = field.shape[0]
    return jnp.concatenate(
        [
            pltpu.roll(field, 1, 0).astype(BF16),
            field.astype(BF16),
            pltpu.roll(field, count - 1, 0).astype(BF16),
        ],
        axis=1,
    )


def cells(ref, begin, lanes=slice(None)):
    return jnp.concatenate(
        [ref[begin + PITCH * r : begin + PITCH * r + 64, lanes] for r in range(8)], axis=0
    )


def transposed(field):
    return field.astype(F32).T.astype(BF16)


def identity():
    shape = (256, 256)
    same = lax.broadcasted_iota(jnp.int32, shape, 0) == lax.broadcasted_iota(jnp.int32, shape, 1)
    return jnp.where(same, 1.0, 0.0).astype(BF16)


def prepare_kernel(bounds, coarse, cot, up, spread, fine3, cot3, skip_share):
    ordered = dot(coarse[...], spread[...]).astype(BF16)
    for r in range(-3, 12):
        j, parity = divmod(r, 2)
        block = dot(up[parity], ordered[(j + 2) * 48 : (j + 2) * 48 + 144])
        begin = (r + 3) * PITCH
        rows = min(PITCH, LENGTH - begin)
        keep = inside(bounds, begin, (rows, 256))
        for k in range(3):
            part = block[k * PITCH : k * PITCH + rows]
            fine3[begin : begin + rows, k * 256 : k * 256 + 256] = jnp.where(keep, part, 0.0).astype(BF16)
    cot3[...] = shifted(cot[...].astype(F32))
    share = dot(transposed(cells(cot, INNER[0])), cells(fine3, INNER[0], slice(256, 512)))
    share = (share * SCALE).astype(BF16)
    skip_share[...] = dot_nt(identity(), share).astype(BF16).reshape(8, 32, 128)


def first_block(weights, k):
    return weights[k // 4, :, k % 4].reshape(256, 128)


def gradient_kernel(
    bounds, weights, fine3, cot3, skip_share, pairs, pairs_t, shares, hidden3, grad_act, second
):
    for k in range(5):
        block = dot(pairs[...], first_block(weights, 10 + k)).astype(BF16)
        second[2 * k] = block[:128]
        second[2 * k + 1] = block[128:]
    begin, end = WIDE
    count = end - begin
    act = jnp.zeros((count, 128), F32)
    for i in range(3):
        kernels = jnp.concatenate([first_block(weights, 3 * i + j) for j in range(3)], axis=0)
        at = begin + PITCH * (i - 1)
        act = act + dot(fine3[at : at + count, :], kernels)
    keep = inside(bounds, begin, (count, 128))
    sigma = jax.nn.sigmoid(act)
    hidden = jnp.where(keep, act * sigma, 0.0)
    hidden3[...] = shifted(hidden)[HIDDEN[0] - begin : HIDDEN[1] - begin]
    grad_hidden = jnp.zeros((count, 128), F32)
    for i in range(3):
        kernels = jnp.concatenate([second[3 * i + 2 - j] for j in range(3)], axis=1)
        at = begin - PITCH * (i - 1)
        grad_hidden = grad_hidden + dot_nt(cot3[at : at + count, :], kernels)
    grad = grad_hidden * sigma * (1.0 + act * (1.0 - sigma))
    grad_act[...] = jnp.where(keep, grad, 0.0).astype(BF16)

    same = identity()
    flipped_grad = transposed(cells(grad_act, INNER[0] - begin))
    for i in range(3):
        share = dot(flipped_grad, cells(fine3, INNER[0] + PITCH * (i - 1)))
        share = (share * SCALE).astype(BF16)
        for j in range(3):
            block = dot_nt(same, share[:, j * 256 : j * 256 + 256]).astype(BF16)
            k = 3 * i + j
            shares[k // 4, :, k % 4] = block.reshape(8, 32, 128)
    shares[2, :, 1] = skip_share[...]
    flipped_cot = transposed(cells(cot3, INNER[0], slice(128, 256)))
    found = []
    for i in range(3):
        share = dot(flipped_cot, cells(hidden3, INNER[0] + PITCH * (i - 1) - HIDDEN[0]))
        share = (share * SCALE).astype(BF16)
        found += [share[:, j * 128 : j * 128 + 128] for j in range(3)]
    found.append(jnp.zeros((128, 128), BF16))
    for k in range(5):
        both = jnp.concatenate(found[2 * k : 2 * k + 2], axis=1)
        block = dot_nt(pairs_t[...], both).astype(BF16)
        b = 10 + k
        shares[b // 4, :, b % 4] = block.reshape(8, 32, 128)
    shares[3, :, 3] = jnp.zeros((8, 32, 128), BF16)


def field_kernel(
    bounds, weights, second, fine3, cot3, hidden3, grad_act, down, spread_t, result, coarse_gradient
):
    skip = first_block(weights, 9)
    begin, end = INNER
    total = dot(fine3[begin:end, 256:512], skip)
    for i in range(3):
        kernels = jnp.concatenate([second[3 * i + j] for j in range(3)], axis=0)
        at = begin + PITCH * (i - 1) - HIDDEN[0]
        total = total + dot(hidden3[at : at + end - begin, :], kernels)
    total = total.astype(BF16)
    for r in range(8):
        result[r] = total[r * PITCH : r * PITCH + 64]

    grad3 = shifted(grad_act[...].astype(F32))
    begin, end = MIDDLE
    count = end - begin
    back = dot_nt(cot3[begin:end, 128:256], skip)
    for i in range(3):
        kernels = jnp.concatenate([first_block(weights, 3 * i + 2 - j) for j in range(3)], axis=1)
        at = begin - PITCH * (i - 1) - WIDE[0]
        back = back + dot_nt(grad3[at : at + count], kernels)
    fine_gradient = jnp.where(inside(bounds, begin, (count, 256)), back, 0.0).astype(BF16)
    for j in range(4):
        part = dot(down[...], fine_gradient[2 * j * PITCH : 2 * j * PITCH + 4 * PITCH + 16])
        coarse_gradient[j] = dot(part.astype(BF16), spread_t[...]).astype(BF16)


def call(kernel, outs, *operands):
    vmem = pl.BlockSpec(memory_space=pltpu.VMEM)
    smem = pl.BlockSpec(memory_space=pltpu.SMEM)
    return pl.pallas_call(
        kernel,
        out_shape=[jax.ShapeDtypeStruct(shape, BF16) for shape in outs],
        in_specs=[smem] + [vmem] * (len(operands) - 1),
        out_specs=[vmem] * len(outs),
        compiler_params=pltpu.CompilerParams(vmem_limit_bytes=40 * 1024 * 1024),
    )(*operands)


def neighbours(low_side, high_side, axis, periodic):
    count = lax.axis_size(axis)
    up = [(i, i + 1) for i in range(count - 1)] + ([(count - 1, 0)] if periodic else [])
    down = [(b, a) for a, b in up]
    return lax.ppermute(high_side, axis, up), lax.ppermute(low_side, axis, down)


def coarse_field(coarse):
    low, high = neighbours(coarse[:2], coarse[-2:], LAT, False)
    tall = jnp.concatenate([low, coarse, high], axis=0)
    left, right = neighbours(tall[:, :2], tall[:, -2:], LON, True)
    gap = jnp.zeros((8, 12, 256), BF16)
    wide = jnp.concatenate([tall, right, gap, left], axis=1)
    return jnp.pad(wide, ((1, 1), (0, 0), (0, 0))).reshape(480, 256)


def cot_field(cotangent):
    low, high = neighbours(cotangent[:3], cotangent[-3:], LAT, False)
    tall = jnp.concatenate([low, cotangent, high], axis=0)
    left, right = neighbours(tall[:, :3], tall[:, -3:], LON, True)
    after = ((0, 1), (0, 0), (0, 0))
    gap = jnp.zeros((15, 10, 128), BF16)
    wide = jnp.concatenate(
        [jnp.pad(right, ((1, 0), (0, 0), (0, 0))), gap, jnp.pad(left, after), jnp.pad(tall, after)],
        axis=1,
    )
    return wide.reshape(15 * PITCH, 128)[:LENGTH]


def gathered(w_first, w_second, w_skip):
    pairs = jnp.pad(w_second.reshape(9, 128), ((0, 3), (0, 0))).reshape(6, 2, 128)
    mine = jnp.concatenate([w_first, w_skip[None], pairs], axis=0)
    piece = lax.dynamic_slice_in_dim(mine, 4 * lax.axis_index(LAT), 4, 0)
    sent = jnp.broadcast_to(piece[None], (16, 4, 2, 128))
    came = lax.all_to_all(sent, "z", 0, 0, tiled=True)
    block = came.transpose(1, 0, 2, 3).reshape(4, 32, 128)
    sent = jnp.broadcast_to(block[None], (32, 4, 32, 128))
    return lax.all_to_all(sent, PLANE, 0, 0, tiled=True).reshape(4, 8, 4, 32, 128)


def summed(shares):
    came = lax.all_to_all(shares.reshape(32, 4, 32, 128), PLANE, 0, 0, tiled=True)
    part = jnp.sum(came.astype(F32), axis=0).astype(BF16)
    part = part.reshape(4, 16, 2, 128).transpose(1, 0, 2, 3)
    sent = jnp.broadcast_to(part[None], (4, 16, 4, 2, 128)).reshape(64, 4, 2, 128)
    came = lax.all_to_all(sent, LAT + ("z",), 0, 0, tiled=True)
    return jnp.sum(came.reshape(4, 16, 4, 2, 128).astype(F32), axis=1).reshape(16, 2, 128)


def on_device(coarse, w_first, w_second, w_skip, cotangent):
    spread, pairs = channel_orders()
    spread, spread_t, pairs, pairs_t, up, down = (
        jnp.asarray(m, BF16)
        for m in (spread, spread.T, pairs, pairs.T, upsampling_matrices(), decimation_matrix())
    )
    lat = lax.axis_index(LAT)
    bounds = jnp.stack([jnp.where(lat == 0, 248, 0), jnp.where(lat == 3, 888, LENGTH)]).astype(jnp.int32)

    weights = gathered(w_first, w_second, w_skip)
    fine3, cot3, skip_share = call(
        prepare_kernel,
        [(LENGTH, 768), (LENGTH, 384), (8, 32, 128)],
        bounds, coarse_field(coarse), cot_field(cotangent), up, spread,
    )
    shares, hidden3, grad_act, second = call(
        gradient_kernel,
        [(4, 8, 4, 32, 128), (HIDDEN[1] - HIDDEN[0], 384), (WIDE[1] - WIDE[0], 128), (10, 128, 128)],
        bounds, weights, fine3, cot3, skip_share, pairs, pairs_t,
    )
    grads = summed(shares)
    result, coarse_gradient = call(
        field_kernel,
        [(8, 64, 128), (4, 32, 256)],
        bounds, weights, second, fine3, cot3, hidden3, grad_act, down, spread_t,
    )
    grad_second = grads[10:15].reshape(10, 1, 128)[:9]
    return result, coarse_gradient, grads[:9], grad_second, grads[9]


def solution(mesh):
    axes = ("xl", "core", "z", "xh", "y")
    fine = Mesh(mesh.devices.reshape(2, 2, 16, 2, 4), axes)
    field, taps, plain = P(LAT, LON, None), P(None, LON, None), P(LON, None)
    return jax.shard_map(
        on_device,
        mesh=fine,
        in_specs=(field, taps, taps, plain, field),
        out_specs=(field, field, taps, taps, plain),
        check_vma=False,
    )
```

```python
import jax
import jax.numpy as jnp
import numpy as np
from jax import lax
from jax.experimental import pallas as pl
from jax.experimental.pallas import tpu as pltpu
from jax.sharding import Mesh, PartitionSpec as P

PITCH = 80
LENGTH = 14 * PITCH + 16
WIDE = (PITCH, 12 * PITCH + 96)
MIDDLE = (2 * PITCH, 12 * PITCH + 16)
HIDDEN = (2 * PITCH + 16, 12 * PITCH)
INNER = (256, 880)
F32 = jnp.float32
BF16 = jnp.bfloat16
SCALE = 1.0 / 512.0
LAT = ("xl", "core")
LON = ("z", "xh", "y")
PLANE = ("xl", "core", "xh", "y")


def upsampling_matrices():
    taps = {}
    for parity in range(2):
        for dc in (-1, 0, 1):
            for u in range(PITCH):
                row, col = (parity - 1, 64 + u + dc) if u < 8 else (parity, u - 16 + dc)
                if not -3 <= col <= 66:
                    continue
                for wr, m in ((0.75, row // 2), (0.25, row // 2 + (1 if row % 2 else -1))):
                    for wc, n in ((0.75, col // 2), (0.25, col // 2 + (1 if col % 2 else -1))):
                        taps[parity, (dc + 1) * PITCH + u, (m + 1) * 48 + n % 48] = wr * wc
    out = np.zeros((2, 3 * PITCH, 144), np.float32)
    for place, weight in taps.items():
        out[place] = weight
    return out


def decimation_matrix():
    out = np.zeros((32, 4 * PITCH + 16), np.float32)
    weights = (0.25, 0.75, 0.75, 0.25)
    for j in range(32):
        for a in range(4):
            for b in range(4):
                out[j, a * PITCH + 16 + 2 * j - 1 + b] = weights[a] * weights[b]
    return out


def spread_row(column):
    return ((column >> 1) & 15) * 16 + (column >> 5) * 2 + (column & 1)


def pair_row(column):
    return (column & 1) * 128 + ((column >> 1) & 15) * 8 + (column >> 5)


def block_row(row):
    return ((row >> 1) & 15) * 8 + (row >> 5) * 2 + (row & 1)


def permutation(size, place, by_column):
    rows = lax.broadcasted_iota(jnp.int32, (size, size), 0)
    columns = lax.broadcasted_iota(jnp.int32, (size, size), 1)
    same = rows == place(columns) if by_column else columns == place(rows)
    return jnp.where(same, 1.0, 0.0).astype(BF16)


def dot(a, b):
    return lax.dot_general(a, b, (((1,), (0,)), ((), ())), preferred_element_type=F32)


def dot_nt(a, b):
    return lax.dot_general(a, b, (((1,), (1,)), ((), ())), preferred_element_type=F32)


def inside(bounds_ref, begin, shape):
    place = lax.broadcasted_iota(jnp.int32, shape, 0) + begin
    return (place >= bounds_ref[0]) & (place < bounds_ref[1])


def shifted(field):
    count = field.shape[0]
    return jnp.concatenate(
        [
            pltpu.roll(field, 1, 0).astype(BF16),
            field.astype(BF16),
            pltpu.roll(field, count - 1, 0).astype(BF16),
        ],
        axis=1,
    )


def cells(ref, begin, lanes=slice(None)):
    return jnp.concatenate(
        [ref[begin + PITCH * r : begin + PITCH * r + 64, lanes] for r in range(8)], axis=0
    )


def transposed(field):
    return field.astype(F32).T.astype(BF16)


def identity():
    return permutation(256, lambda row: row, True)


def copied(pairs, semaphores):
    copies = [pltpu.make_async_copy(a, b, semaphores.at[i]) for i, (a, b) in enumerate(pairs)]
    for copy in copies:
        copy.start()
    return copies


def finish(copies):
    for copy in copies:
        copy.wait()


def pack_kernel(lat, first, second, skip, sent, rows, first_here, second_here, skip_here, semaphores):
    copies = copied([(first, first_here), (second, second_here), (skip, skip_here)], semaphores)
    rows[...] = jnp.zeros((32, 128), F32)
    finish(copies)
    for k in range(9):
        rows[2 * k : 2 * k + 2] = first_here[k].astype(F32)
    rows[20:29] = second_here[...].astype(F32)
    rows[18:20] = skip_here[...].astype(F32)
    piece = rows[pl.ds(pl.multiple_of(lat[0] * 8, 8), 8)].astype(BF16)
    sent[...] = jnp.broadcast_to(piece[None], (16, 8, 128))


def either(flag, a, b):
    return jnp.where(flag, a.astype(F32), b.astype(F32)).astype(BF16)


def exchanged(swap, moves, out_a, out_b, semaphores):
    @pl.when(swap)
    def _():
        finish(copied(moves(out_b, out_a), semaphores))

    @pl.when(jnp.logical_not(swap))
    def _():
        finish(copied(moves(out_a, out_b), semaphores))


def lat_edge_kernel(spots, coarse, cot, out_a, out_b, semaphores):
    def moves(up, down):
        found = []
        for out, first, second in ((up, 5, 2), (down, 0, 0)):
            found.append((cot.at[first : first + 3], out.at[0:3]))
            for h in range(2):
                lanes = slice(128 * h, 128 * h + 128)
                found.append((coarse.at[second : second + 2, :, lanes], out.at[3:5, 32 * h : 32 * h + 32]))
        return found

    exchanged(spots[1] == 1, moves, out_a, out_b, semaphores)


def edge_at(m, h):
    return 16 + 8 * h + m


def lon_edge_kernel(spots, coarse, cot, lat_a, lat_b, out_a, out_b, semaphores):
    def side_by_side(low, high):
        def moves(up, down):
            found = []
            for out, c, w in ((up, 48, 16), (down, 0, 0)):
                wide, narrow = slice(c, c + 16), slice(w, w + 16)
                found.append((cot.at[:, wide], out.at[3:11]))
                found.append((low.at[0:3, wide], out.at[0:3]))
                found.append((high.at[0:3, wide], out.at[11:14]))
                for h in range(2):
                    lanes, part = slice(128 * h, 128 * h + 128), slice(32 * h + w, 32 * h + w + 16)
                    found.append((coarse.at[:, narrow, lanes], out.at[edge_at(0, h) : edge_at(4, h)]))
                    found.append((low.at[3:5, part], out.at[edge_at(-2, h) : edge_at(0, h)]))
                    found.append((high.at[3:5, part], out.at[edge_at(4, h) : edge_at(6, h)]))
            return found

        exchanged(spots[0] == 1, moves, out_a, out_b, semaphores)

    @pl.when(spots[1] == 1)
    def _():
        side_by_side(lat_a, lat_b)

    @pl.when(spots[1] == 0)
    def _():
        side_by_side(lat_b, lat_a)


def spread_kernel(came, sent):
    order = permutation(128, block_row, False)
    block = dot(order, came[...].reshape(128, 128)).astype(BF16)
    sent[...] = jnp.broadcast_to(block[None], (32, 128, 128))


def cot_parts(cot, low, high, left, right, r):
    ref, k = (low, r + 3) if r < 0 else (cot, r) if r < 8 else (high, r - 8)
    return ref[k], left[r + 3], right[r + 3]


def coarse_parts(coarse, low, high, left, right, m, h):
    e = edge_at(m, h)
    if 0 <= m < 4:
        return coarse[m, :, 128 * h : 128 * h + 128], left[e], right[e]
    ref, k = (low, 5 + m) if m < 0 else (high, m - 1)
    return ref[k, 32 * h : 32 * h + 32], left[e], right[e]


def prepare(bounds, coarse, cot, low, high, left, right, up, fine3, cot3, grid, field):
    nearer = lax.broadcasted_iota(jnp.int32, (16, 128), 0) < 8

    def edge(a, b):
        return jnp.where(nearer, a.astype(F32), b.astype(F32))

    grid[0:48] = jnp.zeros((48, 256), BF16)
    grid[432:480] = jnp.zeros((48, 256), BF16)
    for m in range(-2, 6):
        at = (m + 3) * 48
        for h in range(2):
            lanes = slice(128 * h, 128 * h + 128)
            middle, before, after = coarse_parts(coarse, low, high, left, right, m, h)
            grid[at : at + 32, lanes] = middle
            grid[at + 32 : at + 48, lanes] = edge(after, before).astype(BF16)
    after = jnp.zeros((16, 128), BF16)
    for r in range(-3, 11):
        at = (r + 3) * PITCH
        middle, before, following = cot_parts(cot, low, high, left, right, r)
        field[at : at + 16] = edge(after, before)
        field[at + 16 : at + 80] = middle.astype(F32)
        after = following
    field[14 * PITCH :] = edge(after, jnp.zeros((16, 128), BF16))
    cot3[...] = shifted(field[...])

    ordered = dot(grid[...], permutation(256, spread_row, True)).astype(BF16)
    for r in range(-3, 12):
        j, parity = divmod(r, 2)
        block = dot(up[parity], ordered[(j + 2) * 48 : (j + 2) * 48 + 144])
        begin = (r + 3) * PITCH
        rows = min(PITCH, LENGTH - begin)
        keep = inside(bounds, begin, (rows, 256))
        for k in range(3):
            part = block[k * PITCH : k * PITCH + rows]
            fine3[begin : begin + rows, k * 256 : k * 256 + 256] = jnp.where(keep, part, 0.0).astype(BF16)


def plane_sum_kernel(came, sent):
    total = came[0].astype(F32)
    for k in range(1, 32):
        total = total + came[k].astype(F32)
    order = permutation(128, block_row, True)
    block = dot(order, total.astype(BF16)).astype(BF16).reshape(16, 8, 128)
    for k in range(2):
        sent[:, k] = block


def column_sum_kernel(came, total):
    part = came[0].astype(F32)
    for k in range(1, 16):
        part = part + came[k].astype(F32)
    total[...] = part


def final_kernel(core, mine, other, first, second, skip):
    low = core[0] == 0
    pieces = []
    for k in range(2):
        pieces += [jnp.where(low, mine[k], other[k]), jnp.where(low, other[k], mine[k])]
    total = jnp.concatenate(pieces, axis=0)
    for k in range(9):
        first[k] = total[2 * k : 2 * k + 2]
        second[k] = total[20 + k : 21 + k]
    skip[...] = total[18:20]


def first_block(weights, k):
    return weights[k // 4, :, k % 4].reshape(256, 128)


def main_kernel(
    bounds, spots, weights_far, coarse_far, cot_far, lat_a_far, lat_b_far, lon_a_far, lon_b_far, up_far,
    shares_far, second_far, fine_far, cot_kept, hidden_far, grad_far,
    weights, coarse, cot, lat_a, lat_b, lon_a, lon_b, up,
    low, high, left, right, shares, fine3, cot3, grid, field, second, hidden3, grad_act, semaphores,
):
    far = (weights_far, coarse_far, cot_far, lat_a_far, lat_b_far, lon_a_far, lon_b_far, up_far)
    here = (weights, coarse, cot, lat_a, lat_b, lon_a, lon_b, up)
    copies = copied(list(zip(far, here))[::-1], semaphores)
    kept = []

    def send(source, target):
        at = len(copies) + len(kept)
        kept.extend(copied([(source, target)], semaphores.at[at : at + 1]))

    def share_block(b, block):
        shares[b // 4, :, b % 4] = block.astype(BF16).reshape(8, 32, 128)
        send(shares.at[b // 4, :, b % 4], shares_far.at[b // 4, :, b % 4])

    pairs, pairs_t = permutation(256, pair_row, True), permutation(256, pair_row, False)
    same = identity()
    finish(copies[:-1])
    odd, second_core = spots[0] == 1, spots[1] == 1
    left[...] = either(odd, lon_a[...], lon_b[...])
    right[...] = either(odd, lon_b[...], lon_a[...])
    low[...] = either(second_core, lat_a[...], lat_b[...])
    high[...] = either(second_core, lat_b[...], lat_a[...])
    prepare(bounds, coarse, cot, low, high, left, right, up, fine3, cot3, grid, field)
    send(fine3.at[INNER[0] : INNER[1], 256:512], fine_far)
    send(cot3.at[MIDDLE[0] : MIDDLE[1], 128:256], cot_kept)
    flipped_cot = transposed(cells(cot3, INNER[0], slice(128, 256)))
    share = (dot(flipped_cot, cells(fine3, INNER[0], slice(256, 512))) * SCALE).astype(BF16)
    share_block(9, dot_nt(same, share))
    share_block(15, jnp.zeros((256, 128), F32))
    finish(copies[-1:])
    for k in range(5):
        block = dot(pairs, first_block(weights, 10 + k)).astype(BF16)
        second[2 * k] = block[:128]
        second[2 * k + 1] = block[128:]
    send(second, second_far)
    begin, end = WIDE
    count = end - begin
    act = jnp.zeros((count, 128), F32)
    for i in range(3):
        kernels = jnp.concatenate([first_block(weights, 3 * i + j) for j in range(3)], axis=0)
        at = begin + PITCH * (i - 1)
        act = act + dot(fine3[at : at + count, :], kernels)
    keep = inside(bounds, begin, (count, 128))
    sigma = jax.nn.sigmoid(act)
    hidden = jnp.where(keep, act * sigma, 0.0)
    hidden3[...] = shifted(hidden)[HIDDEN[0] - begin : HIDDEN[1] - begin]
    send(hidden3, hidden_far)
    grad_hidden = jnp.zeros((count, 128), F32)
    for i in range(3):
        kernels = jnp.concatenate([second[3 * i + 2 - j] for j in range(3)], axis=1)
        at = begin - PITCH * (i - 1)
        grad_hidden = grad_hidden + dot_nt(cot3[at : at + count, :], kernels)
    grad = grad_hidden * sigma * (1.0 + act * (1.0 - sigma))
    grad_act[...] = jnp.where(keep, grad, 0.0).astype(BF16)
    send(grad_act, grad_far)

    found = []
    for i in range(3):
        share = dot(flipped_cot, cells(hidden3, INNER[0] + PITCH * (i - 1) - HIDDEN[0]))
        share = (share * SCALE).astype(BF16)
        found += [share[:, j * 128 : j * 128 + 128] for j in range(3)]
    found.append(jnp.zeros((128, 128), BF16))
    for k in range(5):
        both = jnp.concatenate(found[2 * k : 2 * k + 2], axis=1)
        share_block(10 + k, dot_nt(pairs_t, both))
    flipped_grad = transposed(cells(grad_act, INNER[0] - begin))
    for i in range(3):
        share = dot(flipped_grad, cells(fine3, INNER[0] + PITCH * (i - 1)))
        share = (share * SCALE).astype(BF16)
        for j in range(3):
            share_block(3 * i + j, dot_nt(same, share[:, j * 256 : j * 256 + 256]))
    finish(kept)


def field_kernel(
    bounds, weights, second, fine, cot, hidden3, grad_act, down, result, coarse_gradient
):
    skip = first_block(weights, 9)
    begin, end = INNER
    total = dot(fine[...], skip)
    for i in range(3):
        kernels = jnp.concatenate([second[3 * i + j] for j in range(3)], axis=0)
        at = begin + PITCH * (i - 1) - HIDDEN[0]
        total = total + dot(hidden3[at : at + end - begin, :], kernels)
    total = total.astype(BF16)
    for r in range(8):
        result[r] = total[r * PITCH : r * PITCH + 64]

    grad3 = shifted(grad_act[...].astype(F32))
    begin, end = MIDDLE
    count = end - begin
    back = dot_nt(cot[...], skip)
    for i in range(3):
        kernels = jnp.concatenate([first_block(weights, 3 * i + 2 - j) for j in range(3)], axis=1)
        at = begin - PITCH * (i - 1) - WIDE[0]
        back = back + dot_nt(grad3[at : at + count], kernels)
    fine_gradient = jnp.where(inside(bounds, begin, (count, 256)), back, 0.0).astype(BF16)
    spread_t = permutation(256, spread_row, False)
    for j in range(4):
        part = dot(down[...], fine_gradient[2 * j * PITCH : 2 * j * PITCH + 4 * PITCH + 16])
        coarse_gradient[j] = dot(part.astype(BF16), spread_t).astype(BF16)


def call(kernel, outs, *operands, spaces="", scratch=(), semaphores=0, dtype=BF16, vmem=16):
    kinds = dict(s=pltpu.SMEM, h=pltpu.HBM, v=pltpu.VMEM)
    specs = [pl.BlockSpec(memory_space=kinds[k]) for k in spaces]
    return pl.pallas_call(
        kernel,
        out_shape=[jax.ShapeDtypeStruct(shape, dtype) for shape in outs],
        in_specs=specs[: len(operands)],
        out_specs=specs[len(operands) :],
        scratch_shapes=[pltpu.VMEM(*s) for s in scratch]
        + ([pltpu.SemaphoreType.DMA((semaphores,))] if semaphores else []),
        compiler_params=pltpu.CompilerParams(vmem_limit_bytes=vmem * 1024 * 1024),
    )(*operands)


def pairwise(first, second, axis, periodic):
    count = lax.axis_size(axis)
    ends = [(i, (i + 1) % count) for i in range(count if periodic else count - 1)]
    steps = [[(a, b), (b, a)] for a, b in ends]
    return (
        lax.ppermute(first, axis, [p for step in steps[0::2] for p in step]),
        lax.ppermute(second, axis, [p for step in steps[1::2] for p in step]),
    )


def on_device(coarse, w_first, w_second, w_skip, cotangent):
    up, down = jnp.asarray(upsampling_matrices(), BF16), jnp.asarray(decimation_matrix(), BF16)
    lat = lax.axis_index(LAT).astype(jnp.int32)
    bounds = jnp.stack([jnp.where(lat == 0, 248, 0), jnp.where(lat == 3, 888, LENGTH)]).astype(jnp.int32)

    spots = jnp.stack([lax.axis_index("y") % 2, lax.axis_index("core")]).astype(jnp.int32)
    (sent,) = call(
        pack_kernel, [(16, 8, 128)], lat[None], w_first, w_second.reshape(9, 128), w_skip,
        spaces="shhhv", vmem=60,
        scratch=[((32, 128), F32), ((9, 2, 128), BF16), ((9, 128), BF16), ((2, 128), BF16)],
        semaphores=3,
    )
    came = lax.all_to_all(sent, "z", 0, 0, tiled=True)
    edges = call(
        lat_edge_kernel, [(5, 64, 128)] * 2, spots, coarse, cotangent,
        spaces="shhvv", semaphores=6, vmem=60,
    )
    lat_a, lat_b = pairwise(*edges, LAT, False)
    came, lat_a, lat_b = lax.optimization_barrier((came, lat_a, lat_b))
    (sent,) = call(spread_kernel, [(32, 128, 128)], came, spaces="vv")
    sent, lat_a, lat_b = lax.optimization_barrier((sent, lat_a, lat_b))
    weights = lax.all_to_all(sent, PLANE, 0, 0, tiled=True).reshape(4, 8, 4, 32, 128)
    edges = call(
        lon_edge_kernel, [(30, 16, 128)] * 2, spots, coarse, cotangent, lat_a, lat_b,
        spaces="shhhhvv", semaphores=18, vmem=60,
    )
    lon_a, lon_b = pairwise(*edges, LON, True)
    blocks = (4, 8, 4, 32, 128)
    kept = [
        (10, 128, 128), (INNER[1] - INNER[0], 256), (MIDDLE[1] - MIDDLE[0], 128),
        (HIDDEN[1] - HIDDEN[0], 384), (WIDE[1] - WIDE[0], 128),
    ]
    shares, second, fine, cot_kept, hidden3, grad_act = call(
        main_kernel, [blocks] + kept,
        bounds, spots, weights, coarse, cotangent, lat_a, lat_b, lon_a, lon_b, up,
        spaces="sshhhhhhhh" + "hhhhhh",
        scratch=[
            (shape, BF16)
            for shape in [
                blocks, (4, 32, 256), (8, 64, 128), (5, 64, 128), (5, 64, 128), (30, 16, 128), (30, 16, 128),
                (2, 240, 144), (5, 64, 128), (5, 64, 128), (30, 16, 128), (30, 16, 128), blocks, (LENGTH, 768), (LENGTH, 384), (480, 256),
            ]
        ]
        + [((LENGTH, 128), F32)]
        + [(shape, BF16) for shape in (kept[0], kept[3], kept[4])],
        semaphores=8 + 5 + 16,
        vmem=60,
    )
    came = lax.all_to_all(shares.reshape(32, 128, 128), PLANE, 0, 0, tiled=True)
    (sent,) = call(plane_sum_kernel, [(16, 2, 8, 128)], came, spaces="vv")
    came = lax.all_to_all(sent.reshape(32, 8, 128), ("z", "xl"), 0, 0, tiled=True)
    result, coarse_gradient = call(
        field_kernel, [(8, 64, 128), (4, 32, 256)],
        bounds, weights, second, fine, cot_kept, hidden3, grad_act, down,
        spaces="svvvvvvvvv",
    )
    came, result, coarse_gradient = lax.optimization_barrier((came, result, coarse_gradient))
    (mine,) = call(column_sum_kernel, [(2, 8, 128)], came.reshape(16, 2, 8, 128), spaces="vv", dtype=F32)
    other = lax.ppermute(mine, "core", [(0, 1), (1, 0)])
    grads = call(
        final_kernel, [(9, 2, 128), (9, 1, 128), (2, 128)],
        lax.axis_index("core").astype(jnp.int32)[None], mine, other,
        spaces="svvvvv", dtype=F32,
    )
    return result, coarse_gradient, *grads


def solution(mesh):
    axes = ("xl", "core", "z", "xh", "y")
    fine = Mesh(mesh.devices.reshape(2, 2, 16, 2, 4), axes)
    field, taps, plain = P(LAT, LON, None), P(None, LON, None), P(LON, None)
    return jax.shard_map(
        on_device,
        mesh=fine,
        in_specs=(field, taps, taps, plain, field),
        out_specs=(field, field, taps, taps, plain),
        check_vma=False,
    )
```

```python
import jax
import jax.numpy as jnp
import numpy as np
from jax import lax
from jax.experimental import pallas as pl
from jax.experimental.pallas import tpu as pltpu
from jax.sharding import Mesh, PartitionSpec as P

PITCH = 80
LENGTH = 14 * PITCH + 16
WIDE = (PITCH, 12 * PITCH + 96)
MIDDLE = (2 * PITCH, 12 * PITCH + 16)
HIDDEN = (2 * PITCH + 16, 12 * PITCH)
INNER = (256, 880)
F32 = jnp.float32
BF16 = jnp.bfloat16
SCALE = 1.0 / 512.0
LAT = ("xl", "core")
LON = ("z", "xh", "y")
PLANE = ("xl", "core", "xh", "y")


def upsampling_matrices():
    taps = {}
    for parity in range(2):
        for dc in (-1, 0, 1):
            for u in range(PITCH):
                row, col = (parity - 1, 64 + u + dc) if u < 8 else (parity, u - 16 + dc)
                if not -3 <= col <= 66:
                    continue
                for wr, m in ((0.75, row // 2), (0.25, row // 2 + (1 if row % 2 else -1))):
                    for wc, n in ((0.75, col // 2), (0.25, col // 2 + (1 if col % 2 else -1))):
                        taps[parity, (dc + 1) * PITCH + u, (m + 1) * 48 + n % 48] = wr * wc
    out = np.zeros((2, 3 * PITCH, 144), np.float32)
    for place, weight in taps.items():
        out[place] = weight
    return out


def decimation_matrix():
    out = np.zeros((32, 4 * PITCH + 16), np.float32)
    weights = (0.25, 0.75, 0.75, 0.25)
    for j in range(32):
        for a in range(4):
            for b in range(4):
                out[j, a * PITCH + 16 + 2 * j - 1 + b] = weights[a] * weights[b]
    return out


def spread_row(column):
    return ((column >> 1) & 15) * 16 + (column >> 5) * 2 + (column & 1)


def pair_row(column):
    return (column & 1) * 128 + ((column >> 1) & 15) * 8 + (column >> 5)


def block_row(row):
    return ((row >> 1) & 15) * 8 + (row >> 5) * 2 + (row & 1)


def permutation(size, place, by_column):
    rows = lax.broadcasted_iota(jnp.int32, (size, size), 0)
    columns = lax.broadcasted_iota(jnp.int32, (size, size), 1)
    same = rows == place(columns) if by_column else columns == place(rows)
    return jnp.where(same, 1.0, 0.0).astype(BF16)


def lat_place():
    return lax.axis_index("xl") * 2 + lax.axis_index("core")


def in_odd_column():
    return lax.rem(lax.axis_index("y"), 2) == 1


def in_second_core():
    return lax.axis_index("core") == 1


def dot(a, b):
    return lax.dot_general(a, b, (((1,), (0,)), ((), ())), preferred_element_type=F32)


def dot_nt(a, b):
    return lax.dot_general(a, b, (((1,), (1,)), ((), ())), preferred_element_type=F32)


def inside(begin, shape):
    lat = lat_place()
    low, high = jnp.where(lat == 0, 248, 0), jnp.where(lat == 3, 888, LENGTH)
    place = lax.broadcasted_iota(jnp.int32, shape, 0) + begin
    return (place >= low) & (place < high)


def shifted(field):
    count = field.shape[0]
    return jnp.concatenate(
        [
            pltpu.roll(field, 1, 0).astype(BF16),
            field.astype(BF16),
            pltpu.roll(field, count - 1, 0).astype(BF16),
        ],
        axis=1,
    )


def cells(ref, begin, lanes=slice(None)):
    return jnp.concatenate(
        [ref[begin + PITCH * r : begin + PITCH * r + 64, lanes] for r in range(8)], axis=0
    )


def transposed(field):
    return field.astype(F32).T.astype(BF16)


def identity():
    return permutation(256, lambda row: row, True)


def copied(pairs, semaphores):
    copies = [pltpu.make_async_copy(a, b, semaphores.at[i]) for i, (a, b) in enumerate(pairs)]
    for copy in copies:
        copy.start()
    return copies


def finish(copies):
    for copy in copies:
        copy.wait()


def either(flag, a, b):
    return jnp.where(flag, a.astype(F32), b.astype(F32)).astype(BF16)


def exchanged(swap, moves, out_a, out_b, semaphores):
    @pl.when(swap)
    def _():
        finish(copied(moves(out_b, out_a), semaphores))

    @pl.when(jnp.logical_not(swap))
    def _():
        finish(copied(moves(out_a, out_b), semaphores))


def front_kernel(
    first, second, skip, coarse, cot, sent, out_a, out_b, rows, first_here, second_here, skip_here, semaphores
):
    def moves(up, down):
        found = []
        for out, r, m in ((up, 5, 2), (down, 0, 0)):
            found.append((cot.at[r : r + 3], out.at[0:3]))
            for h in range(2):
                lanes = slice(128 * h, 128 * h + 128)
                found.append((coarse.at[m : m + 2, :, lanes], out.at[3:5, 32 * h : 32 * h + 32]))
        return found

    copies = copied([(first, first_here), (second, second_here), (skip, skip_here)], semaphores.at[6:9])
    rows[...] = jnp.zeros((32, 128), F32)
    exchanged(in_second_core(), moves, out_a, out_b, semaphores)
    finish(copies)
    for k in range(9):
        rows[2 * k : 2 * k + 2] = first_here[k].astype(F32)
    rows[20:29] = second_here[...].astype(F32)
    rows[18:20] = skip_here[...].astype(F32)
    piece = rows[pl.ds(pl.multiple_of(lat_place() * 8, 8), 8)].astype(BF16)
    sent[...] = jnp.broadcast_to(piece[None], (16, 8, 128))


def edge_at(m, h):
    return 16 + 8 * h + m


def lon_edge_kernel(coarse, cot, lat_a, lat_b, out_a, out_b, low, high):
    odd = in_odd_column()
    sides(lat_a, lat_b, low, high, in_second_core())
    ups, downs = [None] * 30, [None] * 30
    for r in range(-3, 11):
        ref, k = cot_row(cot, low, high, r)
        ups[r + 3] = ref[k, 48:64].astype(F32)[8:]
        downs[r + 3] = ref[k, 0:16].astype(F32)[:8]
    for m in range(-2, 6):
        for h in range(2):
            row = coarse_row(coarse, low, high, m, h).astype(F32)
            ups[edge_at(m, h)] = row[24:32]
            downs[edge_at(m, h)] = row[0:8]
    for k in range(15):
        up = jnp.concatenate(ups[2 * k : 2 * k + 2], axis=0)
        down = jnp.concatenate(downs[2 * k : 2 * k + 2], axis=0)
        out_a[k] = either(odd, down, up)
        out_b[k] = either(odd, up, down)


def sides(first, second, low, high, swap):
    low[...] = either(swap, first[...], second[...])
    high[...] = either(swap, second[...], first[...])


def cot_row(cot, low, high, r):
    return (low, r + 3) if r < 0 else (cot, r) if r < 8 else (high, r - 8)


def coarse_row(coarse, low, high, m, h):
    if 0 <= m < 4:
        return coarse[m, :, 128 * h : 128 * h + 128]
    ref, k = (low, 5 + m) if m < 0 else (high, m - 1)
    return ref[k, 32 * h : 32 * h + 32]


def spread_kernel(came, sent):
    order = permutation(128, block_row, False)
    block = dot(order, came[...].reshape(128, 128)).astype(BF16)
    sent[...] = jnp.broadcast_to(block[None], (32, 128, 128))


def prepare(coarse, cot, low, high, left, right, up, fine3, cot3, grid, field):
    empty = jnp.zeros((8, 128), F32)

    def group(ref, e):
        return ref[e // 2].astype(F32)[8 * (e % 2) : 8 * (e % 2) + 8]

    grid[0:48] = jnp.zeros((48, 256), BF16)
    grid[432:480] = jnp.zeros((48, 256), BF16)
    for m in range(-2, 6):
        at = (m + 3) * 48
        for h in range(2):
            lanes = slice(128 * h, 128 * h + 128)
            middle, e = coarse_row(coarse, low, high, m, h), edge_at(m, h)
            grid[at : at + 32, lanes] = middle
            margin = jnp.concatenate([group(right, e), group(left, e)], axis=0)
            grid[at + 32 : at + 48, lanes] = margin.astype(BF16)
    after = empty
    for r in range(-3, 11):
        at = (r + 3) * PITCH
        ref, k = cot_row(cot, low, high, r)
        field[at : at + 16] = jnp.concatenate([after, group(left, r + 3)], axis=0)
        field[at + 16 : at + 80] = ref[k].astype(F32)
        after = group(right, r + 3)
    field[14 * PITCH :] = jnp.concatenate([after, empty], axis=0)
    cot3[...] = shifted(field[...])

    ordered = dot(grid[...], permutation(256, spread_row, True)).astype(BF16)
    for r in range(-3, 12):
        j, parity = divmod(r, 2)
        block = dot(up[parity], ordered[(j + 2) * 48 : (j + 2) * 48 + 144])
        begin = (r + 3) * PITCH
        rows = min(PITCH, LENGTH - begin)
        keep = inside(begin, (rows, 256))
        for k in range(3):
            part = block[k * PITCH : k * PITCH + rows]
            fine3[begin : begin + rows, k * 256 : k * 256 + 256] = jnp.where(keep, part, 0.0).astype(BF16)


def plane_sum_kernel(came, sent):
    total = came[0].astype(F32)
    for k in range(1, 32):
        total = total + came[k].astype(F32)
    order = permutation(128, block_row, True)
    block = dot(order, total.astype(BF16)).astype(BF16).reshape(16, 8, 128)
    for k in range(2):
        sent[:, k] = block


def column_sum_kernel(came, total):
    part = came[0].astype(F32)
    for k in range(1, 16):
        part = part + came[k].astype(F32)
    total[...] = part


def final_kernel(mine, other, first, second, skip):
    low = jnp.logical_not(in_second_core())
    pieces = []
    for k in range(2):
        pieces += [jnp.where(low, mine[k], other[k]), jnp.where(low, other[k], mine[k])]
    total = jnp.concatenate(pieces, axis=0)
    for k in range(9):
        first[k] = total[2 * k : 2 * k + 2]
        second[k] = total[20 + k : 21 + k]
    skip[...] = total[18:20]


def first_block(weights, k):
    return weights[k // 4, :, k % 4].reshape(256, 128)


def main_kernel(
    weights, coarse, cot, lat_a, lat_b, lon_a, lon_b, up,
    shares, second, fine, cot_kept, hidden3, grad_act,
    low, high, left, right, fine3, cot3, grid, field,
):
    def share_block(b, block):
        shares[b // 4, :, b % 4] = block.astype(BF16).reshape(8, 32, 128)

    pairs, pairs_t = permutation(256, pair_row, True), permutation(256, pair_row, False)
    same = identity()
    sides(lat_a, lat_b, low, high, in_second_core())
    sides(lon_a, lon_b, left, right, in_odd_column())
    prepare(coarse, cot, low, high, left, right, up, fine3, cot3, grid, field)
    fine[...] = fine3[INNER[0] : INNER[1], 256:512]
    cot_kept[...] = cot3[MIDDLE[0] : MIDDLE[1], 128:256]
    flipped_cot = transposed(cells(cot3, INNER[0], slice(128, 256)))
    share = (dot(flipped_cot, cells(fine3, INNER[0], slice(256, 512))) * SCALE).astype(BF16)
    share_block(9, dot_nt(same, share))
    share_block(15, jnp.zeros((256, 128), F32))
    for k in range(5):
        block = dot(pairs, first_block(weights, 10 + k)).astype(BF16)
        second[2 * k] = block[:128]
        second[2 * k + 1] = block[128:]
    begin, end = WIDE
    count = end - begin
    act = jnp.zeros((count, 128), F32)
    for i in range(3):
        kernels = jnp.concatenate([first_block(weights, 3 * i + j) for j in range(3)], axis=0)
        at = begin + PITCH * (i - 1)
        act = act + dot(fine3[at : at + count, :], kernels)
    keep = inside(begin, (count, 128))
    sigma = jax.nn.sigmoid(act)
    hidden = jnp.where(keep, act * sigma, 0.0)
    hidden3[...] = shifted(hidden)[HIDDEN[0] - begin : HIDDEN[1] - begin]
    grad_hidden = jnp.zeros((count, 128), F32)
    for i in range(3):
        kernels = jnp.concatenate([second[3 * i + 2 - j] for j in range(3)], axis=1)
        at = begin - PITCH * (i - 1)
        grad_hidden = grad_hidden + dot_nt(cot3[at : at + count, :], kernels)
    grad = grad_hidden * sigma * (1.0 + act * (1.0 - sigma))
    grad_act[...] = jnp.where(keep, grad, 0.0).astype(BF16)

    found = []
    for i in range(3):
        share = dot(flipped_cot, cells(hidden3, INNER[0] + PITCH * (i - 1) - HIDDEN[0]))
        share = (share * SCALE).astype(BF16)
        found += [share[:, j * 128 : j * 128 + 128] for j in range(3)]
    found.append(jnp.zeros((128, 128), BF16))
    for k in range(5):
        both = jnp.concatenate(found[2 * k : 2 * k + 2], axis=1)
        share_block(10 + k, dot_nt(pairs_t, both))
    flipped_grad = transposed(cells(grad_act, INNER[0] - begin))
    for i in range(3):
        share = dot(flipped_grad, cells(fine3, INNER[0] + PITCH * (i - 1)))
        share = (share * SCALE).astype(BF16)
        for j in range(3):
            share_block(3 * i + j, dot_nt(same, share[:, j * 256 : j * 256 + 256]))


def field_kernel(
    weights, second, fine, cot, hidden3, grad_act, down, result, coarse_gradient
):
    skip = first_block(weights, 9)
    begin, end = INNER
    total = dot(fine[...], skip)
    for i in range(3):
        kernels = jnp.concatenate([second[3 * i + j] for j in range(3)], axis=0)
        at = begin + PITCH * (i - 1) - HIDDEN[0]
        total = total + dot(hidden3[at : at + end - begin, :], kernels)
    total = total.astype(BF16)
    for r in range(8):
        result[r] = total[r * PITCH : r * PITCH + 64]

    grad3 = shifted(grad_act[...].astype(F32))
    begin, end = MIDDLE
    count = end - begin
    back = dot_nt(cot[...], skip)
    for i in range(3):
        kernels = jnp.concatenate([first_block(weights, 3 * i + 2 - j) for j in range(3)], axis=1)
        at = begin - PITCH * (i - 1) - WIDE[0]
        back = back + dot_nt(grad3[at : at + count], kernels)
    fine_gradient = jnp.where(inside(begin, (count, 256)), back, 0.0).astype(BF16)
    spread_t = permutation(256, spread_row, False)
    for j in range(4):
        part = dot(down[...], fine_gradient[2 * j * PITCH : 2 * j * PITCH + 4 * PITCH + 16])
        coarse_gradient[j] = dot(part.astype(BF16), spread_t).astype(BF16)


def call(kernel, outs, *operands, spaces="", scratch=(), semaphores=0, dtype=BF16, vmem=16):
    kinds = dict(h=pltpu.HBM, v=pltpu.VMEM)
    specs = [pl.BlockSpec(memory_space=kinds[k]) for k in spaces]
    return pl.pallas_call(
        kernel,
        out_shape=[jax.ShapeDtypeStruct(shape, dtype) for shape in outs],
        in_specs=specs[: len(operands)],
        out_specs=specs[len(operands) :],
        scratch_shapes=[pltpu.VMEM(*s) for s in scratch]
        + ([pltpu.SemaphoreType.DMA((semaphores,))] if semaphores else []),
        compiler_params=pltpu.CompilerParams(vmem_limit_bytes=vmem * 1024 * 1024),
    )(*operands)


def pairwise(first, second, axis, periodic):
    count = lax.axis_size(axis)
    ends = [(i, (i + 1) % count) for i in range(count if periodic else count - 1)]
    steps = [[(a, b), (b, a)] for a, b in ends]
    return (
        lax.ppermute(first, axis, [p for step in steps[0::2] for p in step]),
        lax.ppermute(second, axis, [p for step in steps[1::2] for p in step]),
    )


def on_device(coarse, w_first, w_second, w_skip, cotangent):
    up, down = jnp.asarray(upsampling_matrices(), BF16), jnp.asarray(decimation_matrix(), BF16)
    sent, *edges = call(
        front_kernel, [(16, 8, 128)] + [(5, 64, 128)] * 2,
        w_first, w_second.reshape(9, 128), w_skip, coarse, cotangent,
        spaces="hhhhhvvv", vmem=60,
        scratch=[((32, 128), F32), ((9, 2, 128), BF16), ((9, 128), BF16), ((2, 128), BF16)],
        semaphores=9,
    )
    came = lax.all_to_all(sent, "z", 0, 0, tiled=True)
    lat_a, lat_b = pairwise(*edges, LAT, False)
    came, lat_a, lat_b = lax.optimization_barrier((came, lat_a, lat_b))
    (sent,) = call(spread_kernel, [(32, 128, 128)], came, spaces="vv")
    sent, lat_a, lat_b = lax.optimization_barrier((sent, lat_a, lat_b))
    weights = lax.all_to_all(sent, PLANE, 0, 0, tiled=True).reshape(4, 8, 4, 32, 128)
    edges = call(
        lon_edge_kernel, [(15, 16, 128)] * 2, coarse, cotangent, lat_a, lat_b,
        spaces="vvvvvv", scratch=[((5, 64, 128), BF16)] * 2,
    )
    lon_a, lon_b = pairwise(*edges, LON, True)
    blocks = (4, 8, 4, 32, 128)
    kept = [
        (10, 128, 128), (INNER[1] - INNER[0], 256), (MIDDLE[1] - MIDDLE[0], 128),
        (HIDDEN[1] - HIDDEN[0], 384), (WIDE[1] - WIDE[0], 128),
    ]
    shares, second, fine, cot_kept, hidden3, grad_act = call(
        main_kernel, [blocks] + kept,
        weights, coarse, cotangent, lat_a, lat_b, lon_a, lon_b, up,
        spaces="v" * 14,
        scratch=[
            (shape, BF16)
            for shape in [
                (5, 64, 128), (5, 64, 128), (15, 16, 128), (15, 16, 128), (LENGTH, 768), (LENGTH, 384), (480, 256),
            ]
        ]
        + [((LENGTH, 128), F32)],
    )
    came = lax.all_to_all(shares.reshape(32, 128, 128), PLANE, 0, 0, tiled=True)
    (sent,) = call(plane_sum_kernel, [(16, 2, 8, 128)], came, spaces="vv")
    came = lax.all_to_all(sent.reshape(32, 8, 128), ("z", "xl"), 0, 0, tiled=True)
    result, coarse_gradient = call(
        field_kernel, [(8, 64, 128), (4, 32, 256)],
        weights, second, fine, cot_kept, hidden3, grad_act, down,
        spaces="vvvvvvvvv",
    )
    came, result, coarse_gradient = lax.optimization_barrier((came, result, coarse_gradient))
    (mine,) = call(column_sum_kernel, [(2, 8, 128)], came.reshape(16, 2, 8, 128), spaces="vv", dtype=F32)
    other = lax.ppermute(mine, "core", [(0, 1), (1, 0)])
    grads = call(
        final_kernel, [(9, 2, 128), (9, 1, 128), (2, 128)],
        mine, other, spaces="vvvvv", dtype=F32,
    )
    return result, coarse_gradient, *grads


def solution(mesh):
    axes = ("xl", "core", "z", "xh", "y")
    fine = Mesh(mesh.devices.reshape(2, 2, 16, 2, 4), axes)
    field, taps, plain = P(LAT, LON, None), P(None, LON, None), P(LON, None)
    return jax.shard_map(
        on_device,
        mesh=fine,
        in_specs=(field, taps, taps, plain, field),
        out_specs=(field, field, taps, taps, plain),
        check_vma=False,
    )
```

```python
import jax
import jax.numpy as jnp
import numpy as np
from jax import lax
from jax.experimental import pallas as pl
from jax.experimental.pallas import tpu as pltpu
from jax.sharding import Mesh, PartitionSpec as P

PITCH = 80
LENGTH = 14 * PITCH + 16
WIDE = (PITCH, 12 * PITCH + 96)
MIDDLE = (2 * PITCH, 12 * PITCH + 16)
HIDDEN = (2 * PITCH + 16, 12 * PITCH)
INNER = (256, 880)
F32 = jnp.float32
BF16 = jnp.bfloat16
SCALE = 1.0 / 512.0
LAT = ("xl", "core")
LON = ("z", "xh", "y")
PLANE = ("xl", "core", "xh", "y")


def upsampling_matrices():
    taps = {}
    for parity in range(2):
        for dc in (-1, 0, 1):
            for u in range(PITCH):
                row, col = (parity - 1, 64 + u + dc) if u < 8 else (parity, u - 16 + dc)
                if not -3 <= col <= 66:
                    continue
                for wr, m in ((0.75, row // 2), (0.25, row // 2 + (1 if row % 2 else -1))):
                    for wc, n in ((0.75, col // 2), (0.25, col // 2 + (1 if col % 2 else -1))):
                        taps[parity, (dc + 1) * PITCH + u, (m + 1) * 48 + n % 48] = wr * wc
    out = np.zeros((2, 3 * PITCH, 144), np.float32)
    for place, weight in taps.items():
        out[place] = weight
    return out


def decimation_matrix():
    out = np.zeros((32, 4 * PITCH + 16), np.float32)
    weights = (0.25, 0.75, 0.75, 0.25)
    for j in range(32):
        for a in range(4):
            for b in range(4):
                out[j, a * PITCH + 16 + 2 * j - 1 + b] = weights[a] * weights[b]
    return out


def spread_row(column):
    return ((column >> 1) & 15) * 16 + (column >> 5) * 2 + (column & 1)


def pair_row(column):
    return (column & 1) * 128 + ((column >> 1) & 15) * 8 + (column >> 5)


def block_row(row):
    return ((row >> 1) & 15) * 8 + (row >> 5) * 2 + (row & 1)


def permutation(size, place, by_column):
    rows = lax.broadcasted_iota(jnp.int32, (size, size), 0)
    columns = lax.broadcasted_iota(jnp.int32, (size, size), 1)
    same = rows == place(columns) if by_column else columns == place(rows)
    return jnp.where(same, 1.0, 0.0).astype(BF16)


def lat_place():
    return lax.axis_index("xl") * 2 + lax.axis_index("core")


def in_odd_column():
    return lax.rem(lax.axis_index("y"), 2) == 1


def in_second_core():
    return lax.axis_index("core") == 1


def dot(a, b):
    return lax.dot_general(a, b, (((1,), (0,)), ((), ())), preferred_element_type=F32)


def dot_nt(a, b):
    return lax.dot_general(a, b, (((1,), (1,)), ((), ())), preferred_element_type=F32)


def inside(begin, shape):
    lat = lat_place()
    low, high = jnp.where(lat == 0, 248, 0), jnp.where(lat == 3, 888, LENGTH)
    place = lax.broadcasted_iota(jnp.int32, shape, 0) + begin
    return (place >= low) & (place < high)


def shifted(field):
    count = field.shape[0]
    return jnp.concatenate(
        [
            pltpu.roll(field, 1, 0).astype(BF16),
            field.astype(BF16),
            pltpu.roll(field, count - 1, 0).astype(BF16),
        ],
        axis=1,
    )


def cells(ref, begin, lanes=slice(None)):
    return jnp.concatenate(
        [ref[begin + PITCH * r : begin + PITCH * r + 64, lanes] for r in range(8)], axis=0
    )


def transposed(field):
    return field.astype(F32).T.astype(BF16)


def identity():
    return permutation(256, lambda row: row, True)


def copied(pairs, semaphores):
    copies = [pltpu.make_async_copy(a, b, semaphores.at[i]) for i, (a, b) in enumerate(pairs)]
    for copy in copies:
        copy.start()
    return copies


def finish(copies):
    for copy in copies:
        copy.wait()


def either(flag, a, b):
    return jnp.where(flag, a.astype(F32), b.astype(F32)).astype(BF16)


def exchanged(swap, moves, out_a, out_b, semaphores):
    @pl.when(swap)
    def _():
        finish(copied(moves(out_b, out_a), semaphores))

    @pl.when(jnp.logical_not(swap))
    def _():
        finish(copied(moves(out_a, out_b), semaphores))


def front_kernel(
    first, second, skip, coarse, cot, sent, out_a, out_b, rows, first_here, second_here, skip_here, semaphores
):
    def moves(up, down):
        found = []
        for out, r, m in ((up, 5, 2), (down, 0, 0)):
            found.append((cot.at[r : r + 3], out.at[0:3]))
            for h in range(2):
                lanes = slice(128 * h, 128 * h + 128)
                found.append((coarse.at[m : m + 2, :, lanes], out.at[3:5, 32 * h : 32 * h + 32]))
        return found

    copies = copied([(first, first_here), (second, second_here), (skip, skip_here)], semaphores.at[6:9])
    rows[...] = jnp.zeros((32, 128), F32)
    exchanged(in_second_core(), moves, out_a, out_b, semaphores)
    finish(copies)
    for k in range(9):
        rows[2 * k : 2 * k + 2] = first_here[k].astype(F32)
    rows[20:29] = second_here[...].astype(F32)
    rows[18:20] = skip_here[...].astype(F32)
    piece = rows[pl.ds(pl.multiple_of(lat_place() * 8, 8), 8)].astype(BF16)
    sent[...] = jnp.broadcast_to(piece[None], (16, 8, 128))


def edge_at(m, h):
    return 16 + 8 * h + m


def lon_edge_kernel(coarse, cot, lat_a, lat_b, out_a, out_b, low, high):
    odd = in_odd_column()
    sides(lat_a, lat_b, low, high, in_second_core())
    ups, downs = [jnp.zeros((4, 128), F32)] * 32, [jnp.zeros((4, 128), F32)] * 32
    for r in range(-3, 11):
        ref, k = cot_row(cot, low, high, r)
        ups[r + 3] = ref[k, 48:64].astype(F32)[12:]
        downs[r + 3] = ref[k, 0:16].astype(F32)[:4]
    for m in range(-2, 6):
        for h in range(2):
            row = coarse_row(coarse, low, high, m, h).astype(F32)
            ups[edge_at(m, h)] = row[28:32]
            downs[edge_at(m, h)] = row[0:4]
    for k in range(8):
        up = jnp.concatenate(ups[4 * k : 4 * k + 4], axis=0)
        down = jnp.concatenate(downs[4 * k : 4 * k + 4], axis=0)
        out_a[k] = either(odd, down, up)
        out_b[k] = either(odd, up, down)


def sides(first, second, low, high, swap):
    low[...] = either(swap, first[...], second[...])
    high[...] = either(swap, second[...], first[...])


def cot_row(cot, low, high, r):
    return (low, r + 3) if r < 0 else (cot, r) if r < 8 else (high, r - 8)


def coarse_row(coarse, low, high, m, h):
    if 0 <= m < 4:
        return coarse[m, :, 128 * h : 128 * h + 128]
    ref, k = (low, 5 + m) if m < 0 else (high, m - 1)
    return ref[k, 32 * h : 32 * h + 32]


def spread_kernel(came, sent):
    order = permutation(128, block_row, False)
    block = dot(order, came[...].reshape(128, 128)).astype(BF16)
    sent[...] = jnp.broadcast_to(block[None], (32, 128, 128))


def prepare(coarse, cot, low, high, left, right, up, fine3, cot3, grid, field):
    empty = jnp.zeros((4, 128), F32)

    def group(ref, e):
        return ref[e // 4].astype(F32)[4 * (e % 4) : 4 * (e % 4) + 4]

    grid[0:48] = jnp.zeros((48, 256), BF16)
    grid[432:480] = jnp.zeros((48, 256), BF16)
    for m in range(-2, 6):
        at = (m + 3) * 48
        for h in range(2):
            lanes = slice(128 * h, 128 * h + 128)
            middle, e = coarse_row(coarse, low, high, m, h), edge_at(m, h)
            grid[at : at + 32, lanes] = middle
            margin = jnp.concatenate([group(right, e), empty, empty, group(left, e)], axis=0)
            grid[at + 32 : at + 48, lanes] = margin.astype(BF16)
    after = empty
    for r in range(-3, 11):
        at = (r + 3) * PITCH
        ref, k = cot_row(cot, low, high, r)
        field[at : at + 16] = jnp.concatenate([after, empty, empty, group(left, r + 3)], axis=0)
        field[at + 16 : at + 80] = ref[k].astype(F32)
        after = group(right, r + 3)
    field[14 * PITCH :] = jnp.concatenate([after, empty, empty, empty], axis=0)
    cot3[...] = shifted(field[...])

    ordered = dot(grid[...], permutation(256, spread_row, True)).astype(BF16)
    for r in range(-3, 12):
        j, parity = divmod(r, 2)
        block = dot(up[parity], ordered[(j + 2) * 48 : (j + 2) * 48 + 144])
        begin = (r + 3) * PITCH
        rows = min(PITCH, LENGTH - begin)
        keep = inside(begin, (rows, 256))
        for k in range(3):
            part = block[k * PITCH : k * PITCH + rows]
            fine3[begin : begin + rows, k * 256 : k * 256 + 256] = jnp.where(keep, part, 0.0).astype(BF16)


def plane_sum_kernel(came, sent):
    total = came[0].astype(F32)
    for k in range(1, 32):
        total = total + came[k].astype(F32)
    order = permutation(128, block_row, True)
    block = dot(order, total.astype(BF16)).astype(BF16).reshape(16, 8, 128)
    for k in range(2):
        sent[:, k] = block


def column_sum_kernel(came, total):
    part = came[0].astype(F32)
    for k in range(1, 16):
        part = part + came[k].astype(F32)
    total[...] = part


def final_kernel(mine, other, first, second, skip):
    low = jnp.logical_not(in_second_core())
    pieces = []
    for k in range(2):
        pieces += [jnp.where(low, mine[k], other[k]), jnp.where(low, other[k], mine[k])]
    total = jnp.concatenate(pieces, axis=0)
    for k in range(9):
        first[k] = total[2 * k : 2 * k + 2]
        second[k] = total[20 + k : 21 + k]
    skip[...] = total[18:20]


def first_block(weights, k):
    return weights[k // 4, :, k % 4].reshape(256, 128)


def main_kernel(
    weights, coarse, cot, lat_a, lat_b, lon_a, lon_b, up,
    shares, second, fine, cot_kept, hidden3, grad_act,
    low, high, left, right, fine3, cot3, grid, field,
):
    def share_block(b, block):
        shares[b // 4, :, b % 4] = block.astype(BF16).reshape(8, 32, 128)

    pairs, pairs_t = permutation(256, pair_row, True), permutation(256, pair_row, False)
    same = identity()
    sides(lat_a, lat_b, low, high, in_second_core())
    sides(lon_a, lon_b, left, right, in_odd_column())
    prepare(coarse, cot, low, high, left, right, up, fine3, cot3, grid, field)
    fine[...] = fine3[INNER[0] : INNER[1], 256:512]
    cot_kept[...] = cot3[MIDDLE[0] : MIDDLE[1], 128:256]
    flipped_cot = transposed(cells(cot3, INNER[0], slice(128, 256)))
    share = (dot(flipped_cot, cells(fine3, INNER[0], slice(256, 512))) * SCALE).astype(BF16)
    share_block(9, dot_nt(same, share))
    share_block(15, jnp.zeros((256, 128), F32))
    for k in range(5):
        block = dot(pairs, first_block(weights, 10 + k)).astype(BF16)
        second[2 * k] = block[:128]
        second[2 * k + 1] = block[128:]
    begin, end = WIDE
    count = end - begin
    act = jnp.zeros((count, 128), F32)
    for i in range(3):
        kernels = jnp.concatenate([first_block(weights, 3 * i + j) for j in range(3)], axis=0)
        at = begin + PITCH * (i - 1)
        act = act + dot(fine3[at : at + count, :], kernels)
    keep = inside(begin, (count, 128))
    sigma = jax.nn.sigmoid(act)
    hidden = jnp.where(keep, act * sigma, 0.0)
    hidden3[...] = shifted(hidden)[HIDDEN[0] - begin : HIDDEN[1] - begin]
    grad_hidden = jnp.zeros((count, 128), F32)
    for i in range(3):
        kernels = jnp.concatenate([second[3 * i + 2 - j] for j in range(3)], axis=1)
        at = begin - PITCH * (i - 1)
        grad_hidden = grad_hidden + dot_nt(cot3[at : at + count, :], kernels)
    grad = grad_hidden * sigma * (1.0 + act * (1.0 - sigma))
    grad_act[...] = jnp.where(keep, grad, 0.0).astype(BF16)

    found = []
    for i in range(3):
        share = dot(flipped_cot, cells(hidden3, INNER[0] + PITCH * (i - 1) - HIDDEN[0]))
        share = (share * SCALE).astype(BF16)
        found += [share[:, j * 128 : j * 128 + 128] for j in range(3)]
    found.append(jnp.zeros((128, 128), BF16))
    for k in range(5):
        both = jnp.concatenate(found[2 * k : 2 * k + 2], axis=1)
        share_block(10 + k, dot_nt(pairs_t, both))
    flipped_grad = transposed(cells(grad_act, INNER[0] - begin))
    for i in range(3):
        share = dot(flipped_grad, cells(fine3, INNER[0] + PITCH * (i - 1)))
        share = (share * SCALE).astype(BF16)
        for j in range(3):
            share_block(3 * i + j, dot_nt(same, share[:, j * 256 : j * 256 + 256]))


def field_kernel(
    weights, second, fine, cot, hidden3, grad_act, down, result, coarse_gradient
):
    skip = first_block(weights, 9)
    begin, end = INNER
    total = dot(fine[...], skip)
    for i in range(3):
        kernels = jnp.concatenate([second[3 * i + j] for j in range(3)], axis=0)
        at = begin + PITCH * (i - 1) - HIDDEN[0]
        total = total + dot(hidden3[at : at + end - begin, :], kernels)
    total = total.astype(BF16)
    for r in range(8):
        result[r] = total[r * PITCH : r * PITCH + 64]

    grad3 = shifted(grad_act[...].astype(F32))
    begin, end = MIDDLE
    count = end - begin
    back = dot_nt(cot[...], skip)
    for i in range(3):
        kernels = jnp.concatenate([first_block(weights, 3 * i + 2 - j) for j in range(3)], axis=1)
        at = begin - PITCH * (i - 1) - WIDE[0]
        back = back + dot_nt(grad3[at : at + count], kernels)
    fine_gradient = jnp.where(inside(begin, (count, 256)), back, 0.0).astype(BF16)
    spread_t = permutation(256, spread_row, False)
    for j in range(4):
        part = dot(down[...], fine_gradient[2 * j * PITCH : 2 * j * PITCH + 4 * PITCH + 16])
        coarse_gradient[j] = dot(part.astype(BF16), spread_t).astype(BF16)


def call(kernel, outs, *operands, spaces="", scratch=(), semaphores=0, dtype=BF16, vmem=16):
    kinds = dict(h=pltpu.HBM, v=pltpu.VMEM)
    specs = [pl.BlockSpec(memory_space=kinds[k]) for k in spaces]
    return pl.pallas_call(
        kernel,
        out_shape=[jax.ShapeDtypeStruct(shape, dtype) for shape in outs],
        in_specs=specs[: len(operands)],
        out_specs=specs[len(operands) :],
        scratch_shapes=[pltpu.VMEM(*s) for s in scratch]
        + ([pltpu.SemaphoreType.DMA((semaphores,))] if semaphores else []),
        compiler_params=pltpu.CompilerParams(vmem_limit_bytes=vmem * 1024 * 1024),
    )(*operands)


def pairwise(first, second, axis, periodic):
    count = lax.axis_size(axis)
    ends = [(i, (i + 1) % count) for i in range(count if periodic else count - 1)]
    steps = [[(a, b), (b, a)] for a, b in ends]
    return (
        lax.ppermute(first, axis, [p for step in steps[0::2] for p in step]),
        lax.ppermute(second, axis, [p for step in steps[1::2] for p in step]),
    )


def on_device(coarse, w_first, w_second, w_skip, cotangent):
    up, down = jnp.asarray(upsampling_matrices(), BF16), jnp.asarray(decimation_matrix(), BF16)
    sent, *edges = call(
        front_kernel, [(16, 8, 128)] + [(5, 64, 128)] * 2,
        w_first, w_second.reshape(9, 128), w_skip, coarse, cotangent,
        spaces="hhhhhvvv", vmem=60,
        scratch=[((32, 128), F32), ((9, 2, 128), BF16), ((9, 128), BF16), ((2, 128), BF16)],
        semaphores=9,
    )
    came = lax.all_to_all(sent, "z", 0, 0, tiled=True)
    lat_a, lat_b = pairwise(*edges, LAT, False)
    (sent,) = call(spread_kernel, [(32, 128, 128)], came, spaces="vv")
    sent, lat_a, lat_b = lax.optimization_barrier((sent, lat_a, lat_b))
    weights = lax.all_to_all(sent, PLANE, 0, 0, tiled=True).reshape(4, 8, 4, 32, 128)
    edges = call(
        lon_edge_kernel, [(8, 16, 128)] * 2, coarse, cotangent, lat_a, lat_b,
        spaces="vvvvvv", scratch=[((5, 64, 128), BF16)] * 2,
    )
    lon_a, lon_b = pairwise(*edges, LON, True)
    blocks = (4, 8, 4, 32, 128)
    kept = [
        (10, 128, 128), (INNER[1] - INNER[0], 256), (MIDDLE[1] - MIDDLE[0], 128),
        (HIDDEN[1] - HIDDEN[0], 384), (WIDE[1] - WIDE[0], 128),
    ]
    shares, second, fine, cot_kept, hidden3, grad_act = call(
        main_kernel, [blocks] + kept,
        weights, coarse, cotangent, lat_a, lat_b, lon_a, lon_b, up,
        spaces="v" * 14,
        scratch=[
            (shape, BF16)
            for shape in [
                (5, 64, 128), (5, 64, 128), (8, 16, 128), (8, 16, 128), (LENGTH, 768), (LENGTH, 384), (480, 256),
            ]
        ]
        + [((LENGTH, 128), F32)],
    )
    came = lax.all_to_all(shares.reshape(32, 128, 128), PLANE, 0, 0, tiled=True)
    (sent,) = call(plane_sum_kernel, [(16, 2, 8, 128)], came, spaces="vv")
    came = lax.all_to_all(sent.reshape(32, 8, 128), ("z", "xl"), 0, 0, tiled=True)
    result, coarse_gradient = call(
        field_kernel, [(8, 64, 128), (4, 32, 256)],
        weights, second, fine, cot_kept, hidden3, grad_act, down,
        spaces="vvvvvvvvv",
    )
    came, result, coarse_gradient = lax.optimization_barrier((came, result, coarse_gradient))
    (mine,) = call(column_sum_kernel, [(2, 8, 128)], came.reshape(16, 2, 8, 128), spaces="vv", dtype=F32)
    other = lax.ppermute(mine, "core", [(0, 1), (1, 0)])
    grads = call(
        final_kernel, [(9, 2, 128), (9, 1, 128), (2, 128)],
        mine, other, spaces="vvvvv", dtype=F32,
    )
    return result, coarse_gradient, *grads


def solution(mesh):
    axes = ("xl", "core", "z", "xh", "y")
    fine = Mesh(mesh.devices.reshape(2, 2, 16, 2, 4), axes)
    field, taps, plain = P(LAT, LON, None), P(None, LON, None), P(LON, None)
    return jax.shard_map(
        on_device,
        mesh=fine,
        in_specs=(field, taps, taps, plain, field),
        out_specs=(field, field, taps, taps, plain),
        check_vma=False,
    )
```

```python
import jax
import jax.numpy as jnp
import numpy as np
from jax import lax
from jax.experimental import pallas as pl
from jax.experimental.pallas import tpu as pltpu
from jax.sharding import Mesh, PartitionSpec as P

PITCH = 80
LENGTH = 14 * PITCH + 16
WIDE = (PITCH, 12 * PITCH + 96)
MIDDLE = (2 * PITCH, 12 * PITCH + 16)
HIDDEN = (2 * PITCH + 16, 12 * PITCH)
INNER = (256, 880)
F32 = jnp.float32
BF16 = jnp.bfloat16
SCALE = 1.0 / 512.0
LAT = ("xl", "core")
LON = ("z", "xh", "y")
PLANE = ("xh", "y", "xl", "core")


def upsampling_matrices():
    taps = {}
    for parity in range(2):
        for dc in (-1, 0, 1):
            for u in range(PITCH):
                row, col = (parity - 1, 64 + u + dc) if u < 8 else (parity, u - 16 + dc)
                if not -3 <= col <= 66:
                    continue
                for wr, m in ((0.75, row // 2), (0.25, row // 2 + (1 if row % 2 else -1))):
                    for wc, n in ((0.75, col // 2), (0.25, col // 2 + (1 if col % 2 else -1))):
                        taps[parity, (dc + 1) * PITCH + u, (m + 1) * 48 + n % 48] = wr * wc
    out = np.zeros((2, 3 * PITCH, 144), np.float32)
    for place, weight in taps.items():
        out[place] = weight
    return out


def decimation_matrix():
    out = np.zeros((32, 4 * PITCH + 16), np.float32)
    weights = (0.25, 0.75, 0.75, 0.25)
    for j in range(32):
        for a in range(4):
            for b in range(4):
                out[j, a * PITCH + 16 + 2 * j - 1 + b] = weights[a] * weights[b]
    return out


def spread_row(column):
    return ((column >> 1) & 15) * 16 + (column >> 5) * 2 + (column & 1)


def pair_row(column):
    return (column & 1) * 128 + ((column >> 1) & 15) * 8 + (column >> 5)


def block_row(row):
    return ((row >> 1) & 15) * 8 + (row >> 5) * 2 + (row & 1)


def permutation(size, place, by_column):
    rows = lax.broadcasted_iota(jnp.int32, (size, size), 0)
    columns = lax.broadcasted_iota(jnp.int32, (size, size), 1)
    same = rows == place(columns) if by_column else columns == place(rows)
    return jnp.where(same, 1.0, 0.0).astype(BF16)


def lat_place():
    return lax.axis_index("xl") * 2 + lax.axis_index("core")


def in_odd_column():
    return lax.rem(lax.axis_index("y"), 2) == 1


def in_second_core():
    return lax.axis_index("core") == 1


def dot(a, b):
    return lax.dot_general(a, b, (((1,), (0,)), ((), ())), preferred_element_type=F32)


def dot_nt(a, b):
    return lax.dot_general(a, b, (((1,), (1,)), ((), ())), preferred_element_type=F32)


def inside(begin, shape):
    lat = lat_place()
    low, high = jnp.where(lat == 0, 248, 0), jnp.where(lat == 3, 888, LENGTH)
    place = lax.broadcasted_iota(jnp.int32, shape, 0) + begin
    return (place >= low) & (place < high)


def shifted(field):
    count = field.shape[0]
    return jnp.concatenate(
        [
            pltpu.roll(field, 1, 0).astype(BF16),
            field.astype(BF16),
            pltpu.roll(field, count - 1, 0).astype(BF16),
        ],
        axis=1,
    )


def cells(ref, begin, lanes=slice(None)):
    return jnp.concatenate(
        [ref[begin + PITCH * r : begin + PITCH * r + 64, lanes] for r in range(8)], axis=0
    )


def transposed(field):
    return field.astype(F32).T.astype(BF16)


def identity():
    return permutation(256, lambda row: row, True)


def copied(pairs, semaphores):
    copies = [pltpu.make_async_copy(a, b, semaphores.at[i]) for i, (a, b) in enumerate(pairs)]
    for copy in copies:
        copy.start()
    return copies


def finish(copies):
    for copy in copies:
        copy.wait()


def either(flag, a, b):
    return jnp.where(flag, a.astype(F32), b.astype(F32)).astype(BF16)


def exchanged(swap, moves, out_a, out_b, semaphores):
    @pl.when(swap)
    def _():
        finish(copied(moves(out_b, out_a), semaphores))

    @pl.when(jnp.logical_not(swap))
    def _():
        finish(copied(moves(out_a, out_b), semaphores))


def front_kernel(
    first, second, skip, coarse, cot, sent, out_a, out_b, rows, first_here, second_here, skip_here, semaphores
):
    def moves(up, down):
        found = []
        for out, r, m in ((up, 5, 2), (down, 0, 0)):
            found.append((cot.at[r : r + 3], out.at[0:3]))
            for h in range(2):
                lanes = slice(128 * h, 128 * h + 128)
                found.append((coarse.at[m : m + 2, :, lanes], out.at[3:5, 32 * h : 32 * h + 32]))
        return found

    copies = copied([(first, first_here), (second, second_here), (skip, skip_here)], semaphores.at[6:9])
    rows[...] = jnp.zeros((32, 128), F32)
    exchanged(in_second_core(), moves, out_a, out_b, semaphores)
    finish(copies)
    for k in range(9):
        rows[2 * k : 2 * k + 2] = first_here[k].astype(F32)
    rows[20:29] = second_here[...].astype(F32)
    rows[18:20] = skip_here[...].astype(F32)
    piece = rows[pl.ds(pl.multiple_of(lat_place() * 8, 8), 8)].astype(BF16)
    sent[...] = jnp.broadcast_to(piece[None], (16, 8, 128))


def edge_at(m, h):
    return 16 + 8 * h + m


def lon_edge_kernel(coarse, cot, lat_a, lat_b, out_a, out_b, low, high):
    odd = in_odd_column()
    sides(lat_a, lat_b, low, high, in_second_core())
    ups, downs = [jnp.zeros((4, 128), F32)] * 32, [jnp.zeros((4, 128), F32)] * 32
    for r in range(-3, 11):
        ref, k = cot_row(cot, low, high, r)
        ups[r + 3] = ref[k, 48:64].astype(F32)[12:]
        downs[r + 3] = ref[k, 0:16].astype(F32)[:4]
    for m in range(-2, 6):
        for h in range(2):
            row = coarse_row(coarse, low, high, m, h).astype(F32)
            ups[edge_at(m, h)] = row[28:32]
            downs[edge_at(m, h)] = row[0:4]
    for k in range(8):
        up = jnp.concatenate(ups[4 * k : 4 * k + 4], axis=0)
        down = jnp.concatenate(downs[4 * k : 4 * k + 4], axis=0)
        out_a[k] = either(odd, down, up)
        out_b[k] = either(odd, up, down)


def sides(first, second, low, high, swap):
    low[...] = either(swap, first[...], second[...])
    high[...] = either(swap, second[...], first[...])


def cot_row(cot, low, high, r):
    return (low, r + 3) if r < 0 else (cot, r) if r < 8 else (high, r - 8)


def coarse_row(coarse, low, high, m, h):
    if 0 <= m < 4:
        return coarse[m, :, 128 * h : 128 * h + 128]
    ref, k = (low, 5 + m) if m < 0 else (high, m - 1)
    return ref[k, 32 * h : 32 * h + 32]


def spread_kernel(came, sent):
    order = permutation(128, block_row, False)
    block = dot(order, came[...].reshape(128, 128)).astype(BF16)
    sent[...] = jnp.broadcast_to(block[None], (32, 128, 128))


def prepare(coarse, cot, low, high, left, right, up, fine3, cot3, grid, field):
    empty = jnp.zeros((4, 128), F32)

    def group(ref, e):
        return ref[e // 4].astype(F32)[4 * (e % 4) : 4 * (e % 4) + 4]

    grid[0:48] = jnp.zeros((48, 256), BF16)
    grid[432:480] = jnp.zeros((48, 256), BF16)
    for m in range(-2, 6):
        at = (m + 3) * 48
        for h in range(2):
            lanes = slice(128 * h, 128 * h + 128)
            middle, e = coarse_row(coarse, low, high, m, h), edge_at(m, h)
            grid[at : at + 32, lanes] = middle
            margin = jnp.concatenate([group(right, e), empty, empty, group(left, e)], axis=0)
            grid[at + 32 : at + 48, lanes] = margin.astype(BF16)
    after = empty
    for r in range(-3, 11):
        at = (r + 3) * PITCH
        ref, k = cot_row(cot, low, high, r)
        field[at : at + 16] = jnp.concatenate([after, empty, empty, group(left, r + 3)], axis=0)
        field[at + 16 : at + 80] = ref[k].astype(F32)
        after = group(right, r + 3)
    field[14 * PITCH :] = jnp.concatenate([after, empty, empty, empty], axis=0)
    cot3[...] = shifted(field[...])

    ordered = dot(grid[...], permutation(256, spread_row, True)).astype(BF16)
    for r in range(-3, 12):
        j, parity = divmod(r, 2)
        block = dot(up[parity], ordered[(j + 2) * 48 : (j + 2) * 48 + 144])
        begin = (r + 3) * PITCH
        rows = min(PITCH, LENGTH - begin)
        keep = inside(begin, (rows, 256))
        for k in range(3):
            part = block[k * PITCH : k * PITCH + rows]
            fine3[begin : begin + rows, k * 256 : k * 256 + 256] = jnp.where(keep, part, 0.0).astype(BF16)


def plane_sum_kernel(came, sent):
    total = came[0].astype(F32)
    for k in range(1, 32):
        total = total + came[k].astype(F32)
    order = permutation(128, block_row, True)
    block = dot(order, total.astype(BF16)).astype(BF16).reshape(16, 8, 128)
    for k in range(2):
        sent[:, k] = block


def column_sum_kernel(came, total):
    part = came[0].astype(F32)
    for k in range(1, 16):
        part = part + came[k].astype(F32)
    total[...] = part


def final_kernel(mine, other, first, second, skip):
    low = jnp.logical_not(in_second_core())
    pieces = []
    for k in range(2):
        pieces += [jnp.where(low, mine[k], other[k]), jnp.where(low, other[k], mine[k])]
    total = jnp.concatenate(pieces, axis=0)
    for k in range(9):
        first[k] = total[2 * k : 2 * k + 2]
        second[k] = total[20 + k : 21 + k]
    skip[...] = total[18:20]


def first_block(weights, k):
    return weights[:, k // 4, k % 4].reshape(256, 128)


def main_kernel(
    weights, coarse, cot, lat_a, lat_b, lon_a, lon_b, up,
    shares, second, fine, cot_kept, hidden3, grad_act,
    low, high, left, right, fine3, cot3, grid, field,
):
    def share_block(b, block):
        shares[:, b // 4, b % 4] = block.astype(BF16).reshape(8, 32, 128)

    pairs, pairs_t = permutation(256, pair_row, True), permutation(256, pair_row, False)
    same = identity()
    sides(lat_a, lat_b, low, high, in_second_core())
    sides(lon_a, lon_b, left, right, in_odd_column())
    prepare(coarse, cot, low, high, left, right, up, fine3, cot3, grid, field)
    fine[...] = fine3[INNER[0] : INNER[1], 256:512]
    cot_kept[...] = cot3[MIDDLE[0] : MIDDLE[1], 128:256]
    flipped_cot = transposed(cells(cot3, INNER[0], slice(128, 256)))
    share = (dot(flipped_cot, cells(fine3, INNER[0], slice(256, 512))) * SCALE).astype(BF16)
    share_block(9, dot_nt(same, share))
    share_block(15, jnp.zeros((256, 128), F32))
    for k in range(5):
        block = dot(pairs, first_block(weights, 10 + k)).astype(BF16)
        second[2 * k] = block[:128]
        second[2 * k + 1] = block[128:]
    begin, end = WIDE
    count = end - begin
    act = jnp.zeros((count, 128), F32)
    for i in range(3):
        kernels = jnp.concatenate([first_block(weights, 3 * i + j) for j in range(3)], axis=0)
        at = begin + PITCH * (i - 1)
        act = act + dot(fine3[at : at + count, :], kernels)
    keep = inside(begin, (count, 128))
    sigma = jax.nn.sigmoid(act)
    hidden = jnp.where(keep, act * sigma, 0.0)
    hidden3[...] = shifted(hidden)[HIDDEN[0] - begin : HIDDEN[1] - begin]
    grad_hidden = jnp.zeros((count, 128), F32)
    for i in range(3):
        kernels = jnp.concatenate([second[3 * i + 2 - j] for j in range(3)], axis=1)
        at = begin - PITCH * (i - 1)
        grad_hidden = grad_hidden + dot_nt(cot3[at : at + count, :], kernels)
    grad = grad_hidden * sigma * (1.0 + act * (1.0 - sigma))
    grad_act[...] = jnp.where(keep, grad, 0.0).astype(BF16)

    found = []
    for i in range(3):
        share = dot(flipped_cot, cells(hidden3, INNER[0] + PITCH * (i - 1) - HIDDEN[0]))
        share = (share * SCALE).astype(BF16)
        found += [share[:, j * 128 : j * 128 + 128] for j in range(3)]
    found.append(jnp.zeros((128, 128), BF16))
    for k in range(5):
        both = jnp.concatenate(found[2 * k : 2 * k + 2], axis=1)
        share_block(10 + k, dot_nt(pairs_t, both))
    flipped_grad = transposed(cells(grad_act, INNER[0] - begin))
    for i in range(3):
        share = dot(flipped_grad, cells(fine3, INNER[0] + PITCH * (i - 1)))
        share = (share * SCALE).astype(BF16)
        for j in range(3):
            share_block(3 * i + j, dot_nt(same, share[:, j * 256 : j * 256 + 256]))


def field_kernel(
    weights, second, fine, cot, hidden3, grad_act, down, result, coarse_gradient
):
    skip = first_block(weights, 9)
    begin, end = INNER
    total = dot(fine[...], skip)
    for i in range(3):
        kernels = jnp.concatenate([second[3 * i + j] for j in range(3)], axis=0)
        at = begin + PITCH * (i - 1) - HIDDEN[0]
        total = total + dot(hidden3[at : at + end - begin, :], kernels)
    total = total.astype(BF16)
    for r in range(8):
        result[r] = total[r * PITCH : r * PITCH + 64]

    grad3 = shifted(grad_act[...].astype(F32))
    begin, end = MIDDLE
    count = end - begin
    back = dot_nt(cot[...], skip)
    for i in range(3):
        kernels = jnp.concatenate([first_block(weights, 3 * i + 2 - j) for j in range(3)], axis=1)
        at = begin - PITCH * (i - 1) - WIDE[0]
        back = back + dot_nt(grad3[at : at + count], kernels)
    fine_gradient = jnp.where(inside(begin, (count, 256)), back, 0.0).astype(BF16)
    spread_t = permutation(256, spread_row, False)
    for j in range(4):
        part = dot(down[...], fine_gradient[2 * j * PITCH : 2 * j * PITCH + 4 * PITCH + 16])
        coarse_gradient[j] = dot(part.astype(BF16), spread_t).astype(BF16)


def call(kernel, outs, *operands, spaces="", scratch=(), semaphores=0, dtype=BF16, vmem=16):
    kinds = dict(h=pltpu.HBM, v=pltpu.VMEM)
    specs = [pl.BlockSpec(memory_space=kinds[k]) for k in spaces]
    return pl.pallas_call(
        kernel,
        out_shape=[jax.ShapeDtypeStruct(shape, dtype) for shape in outs],
        in_specs=specs[: len(operands)],
        out_specs=specs[len(operands) :],
        scratch_shapes=[pltpu.VMEM(*s) for s in scratch]
        + ([pltpu.SemaphoreType.DMA((semaphores,))] if semaphores else []),
        compiler_params=pltpu.CompilerParams(vmem_limit_bytes=vmem * 1024 * 1024),
    )(*operands)


def pairwise(first, second, axis, periodic):
    count = lax.axis_size(axis)
    ends = [(i, (i + 1) % count) for i in range(count if periodic else count - 1)]
    steps = [[(a, b), (b, a)] for a, b in ends]
    return (
        lax.ppermute(first, axis, [p for step in steps[0::2] for p in step]),
        lax.ppermute(second, axis, [p for step in steps[1::2] for p in step]),
    )


def on_device(coarse, w_first, w_second, w_skip, cotangent):
    up, down = jnp.asarray(upsampling_matrices(), BF16), jnp.asarray(decimation_matrix(), BF16)
    sent, *edges = call(
        front_kernel, [(16, 8, 128)] + [(5, 64, 128)] * 2,
        w_first, w_second.reshape(9, 128), w_skip, coarse, cotangent,
        spaces="hhhhhvvv", vmem=60,
        scratch=[((32, 128), F32), ((9, 2, 128), BF16), ((9, 128), BF16), ((2, 128), BF16)],
        semaphores=9,
    )
    came = lax.all_to_all(sent, "z", 0, 0, tiled=True)
    lat_a, lat_b = pairwise(*edges, LAT, False)
    (sent,) = call(spread_kernel, [(32, 128, 128)], came, spaces="vv")
    sent, lat_a, lat_b = lax.optimization_barrier((sent, lat_a, lat_b))
    weights = lax.all_to_all(sent, PLANE, 0, 0, tiled=True).reshape(8, 4, 4, 32, 128)
    edges = call(
        lon_edge_kernel, [(8, 16, 128)] * 2, coarse, cotangent, lat_a, lat_b,
        spaces="vvvvvv", scratch=[((5, 64, 128), BF16)] * 2,
    )
    lon_a, lon_b = pairwise(*edges, LON, True)
    blocks = (8, 4, 4, 32, 128)
    kept = [
        (10, 128, 128), (INNER[1] - INNER[0], 256), (MIDDLE[1] - MIDDLE[0], 128),
        (HIDDEN[1] - HIDDEN[0], 384), (WIDE[1] - WIDE[0], 128),
    ]
    shares, second, fine, cot_kept, hidden3, grad_act = call(
        main_kernel, [blocks] + kept,
        weights, coarse, cotangent, lat_a, lat_b, lon_a, lon_b, up,
        spaces="v" * 14,
        scratch=[
            (shape, BF16)
            for shape in [
                (5, 64, 128), (5, 64, 128), (8, 16, 128), (8, 16, 128), (LENGTH, 768), (LENGTH, 384), (480, 256),
            ]
        ]
        + [((LENGTH, 128), F32)],
    )
    came = lax.all_to_all(shares.reshape(32, 128, 128), PLANE, 0, 0, tiled=True)
    (sent,) = call(plane_sum_kernel, [(16, 2, 8, 128)], came, spaces="vv")
    came = lax.all_to_all(sent.reshape(32, 8, 128), ("z", "xl"), 0, 0, tiled=True)
    result, coarse_gradient = call(
        field_kernel, [(8, 64, 128), (4, 32, 256)],
        weights, second, fine, cot_kept, hidden3, grad_act, down,
        spaces="vvvvvvvvv",
    )
    came, result, coarse_gradient = lax.optimization_barrier((came, result, coarse_gradient))
    (mine,) = call(column_sum_kernel, [(2, 8, 128)], came.reshape(16, 2, 8, 128), spaces="vv", dtype=F32)
    other = lax.ppermute(mine, "core", [(0, 1), (1, 0)])
    grads = call(
        final_kernel, [(9, 2, 128), (9, 1, 128), (2, 128)],
        mine, other, spaces="vvvvv", dtype=F32,
    )
    return result, coarse_gradient, *grads


def solution(mesh):
    axes = ("xl", "core", "z", "xh", "y")
    fine = Mesh(mesh.devices.reshape(2, 2, 16, 2, 4), axes)
    field, taps, plain = P(LAT, LON, None), P(None, LON, None), P(LON, None)
    return jax.shard_map(
        on_device,
        mesh=fine,
        in_specs=(field, taps, taps, plain, field),
        out_specs=(field, field, taps, taps, plain),
        check_vma=False,
    )
```

```python
import jax
import jax.numpy as jnp
import numpy as np
from jax import lax
from jax.experimental import pallas as pl
from jax.experimental.pallas import tpu as pltpu
from jax.sharding import Mesh, PartitionSpec as P

PITCH = 80
LENGTH = 14 * PITCH + 16
WIDE = (PITCH, 12 * PITCH + 96)
MIDDLE = (2 * PITCH, 12 * PITCH + 16)
HIDDEN = (2 * PITCH + 16, 12 * PITCH)
INNER = (256, 880)
F32 = jnp.float32
BF16 = jnp.bfloat16
SCALE = 1.0 / 512.0
LAT = ("xl", "core")
LON = ("z", "xh", "y")
PLANE = ("xh", "y", "xl", "core")


def upsampling_matrices():
    taps = {}
    for parity in range(2):
        for dc in (-1, 0, 1):
            for u in range(PITCH):
                row, col = (parity - 1, 64 + u + dc) if u < 8 else (parity, u - 16 + dc)
                if not -3 <= col <= 66:
                    continue
                for wr, m in ((0.75, row // 2), (0.25, row // 2 + (1 if row % 2 else -1))):
                    for wc, n in ((0.75, col // 2), (0.25, col // 2 + (1 if col % 2 else -1))):
                        taps[parity, (dc + 1) * PITCH + u, (m + 1) * 48 + n % 48] = wr * wc
    out = np.zeros((2, 3 * PITCH, 144), np.float32)
    for place, weight in taps.items():
        out[place] = weight
    return out


def decimation_matrix():
    out = np.zeros((32, 4 * PITCH + 16), np.float32)
    weights = (0.25, 0.75, 0.75, 0.25)
    for j in range(32):
        for a in range(4):
            for b in range(4):
                out[j, a * PITCH + 16 + 2 * j - 1 + b] = weights[a] * weights[b]
    return out


def spread_row(column):
    return ((column >> 1) & 15) * 16 + (column >> 5) * 2 + (column & 1)


def pair_row(column):
    return (column & 1) * 128 + ((column >> 1) & 15) * 8 + (column >> 5)


def block_row(row):
    return ((row >> 1) & 15) * 8 + (row >> 5) * 2 + (row & 1)


def permutation(size, place, by_column):
    rows = lax.broadcasted_iota(jnp.int32, (size, size), 0)
    columns = lax.broadcasted_iota(jnp.int32, (size, size), 1)
    same = rows == place(columns) if by_column else columns == place(rows)
    return jnp.where(same, 1.0, 0.0).astype(BF16)


def lat_place():
    return lax.axis_index("xl") * 2 + lax.axis_index("core")


def in_odd_column():
    return lax.rem(lax.axis_index("y"), 2) == 1


def in_second_core():
    return lax.axis_index("core") == 1


def dot(a, b):
    return lax.dot_general(a, b, (((1,), (0,)), ((), ())), preferred_element_type=F32)


def dot_nt(a, b):
    return lax.dot_general(a, b, (((1,), (1,)), ((), ())), preferred_element_type=F32)


def inside(begin, shape):
    lat = lat_place()
    low, high = jnp.where(lat == 0, 248, 0), jnp.where(lat == 3, 888, LENGTH)
    place = lax.broadcasted_iota(jnp.int32, shape, 0) + begin
    return (place >= low) & (place < high)


def shifted(field):
    count = field.shape[0]
    return jnp.concatenate(
        [
            pltpu.roll(field, 1, 0).astype(BF16),
            field.astype(BF16),
            pltpu.roll(field, count - 1, 0).astype(BF16),
        ],
        axis=1,
    )


def cells(ref, begin, lanes=slice(None)):
    return jnp.concatenate(
        [ref[begin + PITCH * r : begin + PITCH * r + 64, lanes] for r in range(8)], axis=0
    )


def transposed(field):
    return field.astype(F32).T.astype(BF16)


def identity():
    return permutation(256, lambda row: row, True)


def copied(pairs, semaphores):
    copies = [pltpu.make_async_copy(a, b, semaphores.at[i]) for i, (a, b) in enumerate(pairs)]
    for copy in copies:
        copy.start()
    return copies


def finish(copies):
    for copy in copies:
        copy.wait()


def either(flag, a, b):
    return jnp.where(flag, a.astype(F32), b.astype(F32)).astype(BF16)


def exchanged(swap, moves, out_a, out_b, semaphores):
    @pl.when(swap)
    def _():
        finish(copied(moves(out_b, out_a), semaphores))

    @pl.when(jnp.logical_not(swap))
    def _():
        finish(copied(moves(out_a, out_b), semaphores))


def front_kernel(
    first, second, skip, coarse, cot, sent, out_a, out_b, rows, first_here, second_here, skip_here, semaphores
):
    def moves(up, down):
        found = []
        for out, r, m in ((up, 5, 2), (down, 0, 0)):
            found.append((cot.at[r : r + 3], out.at[0:3]))
            for h in range(2):
                lanes = slice(128 * h, 128 * h + 128)
                found.append((coarse.at[m : m + 2, :, lanes], out.at[3:5, 32 * h : 32 * h + 32]))
        return found

    copies = copied([(first, first_here), (second, second_here), (skip, skip_here)], semaphores.at[6:9])
    rows[...] = jnp.zeros((32, 128), F32)
    exchanged(in_second_core(), moves, out_a, out_b, semaphores)
    finish(copies)
    for k in range(9):
        rows[2 * k : 2 * k + 2] = first_here[k].astype(F32)
    rows[20:29] = second_here[...].astype(F32)
    rows[18:20] = skip_here[...].astype(F32)
    piece = rows[pl.ds(pl.multiple_of(lat_place() * 8, 8), 8)].astype(BF16)
    sent[...] = jnp.broadcast_to(piece[None], (16, 8, 128))


def edge_at(m, h):
    return 16 + 8 * h + m


def lon_edge_kernel(coarse, cot, lat_a, lat_b, out_a, out_b, low, high):
    odd = in_odd_column()
    sides(lat_a, lat_b, low, high, in_second_core())
    ups, downs = [jnp.zeros((4, 128), F32)] * 32, [jnp.zeros((4, 128), F32)] * 32
    for r in range(-3, 11):
        ref, k = cot_row(cot, low, high, r)
        ups[r + 3] = ref[k, 48:64].astype(F32)[12:]
        downs[r + 3] = ref[k, 0:16].astype(F32)[:4]
    for m in range(-2, 6):
        for h in range(2):
            row = coarse_row(coarse, low, high, m, h).astype(F32)
            ups[edge_at(m, h)] = row[28:32]
            downs[edge_at(m, h)] = row[0:4]
    for k in range(8):
        up = jnp.concatenate(ups[4 * k : 4 * k + 4], axis=0)
        down = jnp.concatenate(downs[4 * k : 4 * k + 4], axis=0)
        out_a[k] = either(odd, down, up)
        out_b[k] = either(odd, up, down)


def sides(first, second, low, high, swap):
    low[...] = either(swap, first[...], second[...])
    high[...] = either(swap, second[...], first[...])


def cot_row(cot, low, high, r):
    return (low, r + 3) if r < 0 else (cot, r) if r < 8 else (high, r - 8)


def coarse_row(coarse, low, high, m, h):
    if 0 <= m < 4:
        return coarse[m, :, 128 * h : 128 * h + 128]
    ref, k = (low, 5 + m) if m < 0 else (high, m - 1)
    return ref[k, 32 * h : 32 * h + 32]


def spread_kernel(came, sent):
    order = permutation(128, block_row, False)
    block = dot(order, came[...].reshape(128, 128)).astype(BF16)
    sent[...] = jnp.broadcast_to(block[None], (32, 128, 128))


def prepare(coarse, cot, low, high, left, right, up, fine3, cot3, grid, field):
    empty = jnp.zeros((4, 128), F32)

    def group(ref, e):
        return ref[e // 4].astype(F32)[4 * (e % 4) : 4 * (e % 4) + 4]

    grid[0:48] = jnp.zeros((48, 256), BF16)
    grid[432:480] = jnp.zeros((48, 256), BF16)
    for m in range(-2, 6):
        at = (m + 3) * 48
        for h in range(2):
            lanes = slice(128 * h, 128 * h + 128)
            middle, e = coarse_row(coarse, low, high, m, h), edge_at(m, h)
            grid[at : at + 32, lanes] = middle
            margin = jnp.concatenate([group(right, e), empty, empty, group(left, e)], axis=0)
            grid[at + 32 : at + 48, lanes] = margin.astype(BF16)
    after = empty
    for r in range(-3, 11):
        at = (r + 3) * PITCH
        ref, k = cot_row(cot, low, high, r)
        field[at : at + 16] = jnp.concatenate([after, empty, empty, group(left, r + 3)], axis=0)
        field[at + 16 : at + 80] = ref[k].astype(F32)
        after = group(right, r + 3)
    field[14 * PITCH :] = jnp.concatenate([after, empty, empty, empty], axis=0)
    cot3[...] = shifted(field[...])

    ordered = dot(grid[...], permutation(256, spread_row, True)).astype(BF16)
    for r in range(-3, 12):
        j, parity = divmod(r, 2)
        block = dot(up[parity], ordered[(j + 2) * 48 : (j + 2) * 48 + 144])
        begin = (r + 3) * PITCH
        rows = min(PITCH, LENGTH - begin)
        keep = inside(begin, (rows, 256))
        for k in range(3):
            part = block[k * PITCH : k * PITCH + rows]
            fine3[begin : begin + rows, k * 256 : k * 256 + 256] = jnp.where(keep, part, 0.0).astype(BF16)


def plane_sum_kernel(came, sent):
    total = came[0].astype(F32)
    for k in range(1, 32):
        total = total + came[k].astype(F32)
    order = permutation(128, block_row, True)
    block = dot(order, total.astype(BF16)).astype(BF16).reshape(16, 8, 128)
    for k in range(2):
        sent[:, k] = block


def column_sum_kernel(came, total):
    part = came[0].astype(F32)
    for k in range(1, 16):
        part = part + came[k].astype(F32)
    total[...] = part


def final_kernel(mine, other, first, second, skip):
    low = jnp.logical_not(in_second_core())
    pieces = []
    for k in range(2):
        pieces += [jnp.where(low, mine[k], other[k]), jnp.where(low, other[k], mine[k])]
    total = jnp.concatenate(pieces, axis=0)
    for k in range(9):
        first[k] = total[2 * k : 2 * k + 2]
        second[k] = total[20 + k : 21 + k]
    skip[...] = total[18:20]


def first_block(weights, k):
    return weights[:, k // 4, k % 4].reshape(256, 128)


def main_kernel(
    weights, coarse, cot, lat_a, lat_b, lon_a, lon_b, up,
    shares, second, fine, cot_kept, hidden3, grad_act,
    low, high, left, right, fine3, cot3, grid, field,
):
    def share_block(b, block):
        shares[:, b // 4, b % 4] = block.astype(BF16).reshape(8, 32, 128)

    pairs, pairs_t = permutation(256, pair_row, True), permutation(256, pair_row, False)
    same = identity()
    sides(lat_a, lat_b, low, high, in_second_core())
    sides(lon_a, lon_b, left, right, in_odd_column())
    prepare(coarse, cot, low, high, left, right, up, fine3, cot3, grid, field)
    fine[...] = fine3[INNER[0] : INNER[1], 256:512]
    cot_kept[...] = cot3[MIDDLE[0] : MIDDLE[1], 128:256]
    flipped_cot = transposed(cells(cot3, INNER[0], slice(128, 256)))
    share = (dot(flipped_cot, cells(fine3, INNER[0], slice(256, 512))) * SCALE).astype(BF16)
    share_block(9, dot_nt(same, share))
    share_block(15, jnp.zeros((256, 128), F32))
    for k in range(5):
        block = dot(pairs, first_block(weights, 10 + k)).astype(BF16)
        second[2 * k] = block[:128]
        second[2 * k + 1] = block[128:]
    begin, end = WIDE
    count = end - begin
    rows = [
        jnp.concatenate([first_block(weights, 3 * i + j) for j in range(3)], axis=0) for i in range(3)
    ]
    both = dot(fine3[0 : count + PITCH, :], jnp.concatenate(rows[:2], axis=1))
    act = both[:count, :128] + both[PITCH:, 128:]
    act = act + dot(fine3[2 * PITCH : 2 * PITCH + count, :], rows[2])
    keep = inside(begin, (count, 128))
    sigma = jax.nn.sigmoid(act)
    hidden = jnp.where(keep, act * sigma, 0.0)
    hidden3[...] = shifted(hidden)[HIDDEN[0] - begin : HIDDEN[1] - begin]
    rows = [jnp.concatenate([second[3 * i + 2 - j] for j in range(3)], axis=1) for i in range(3)]
    both = dot_nt(cot3[0 : count + PITCH, :], jnp.concatenate(rows[1:], axis=0))
    grad_hidden = both[PITCH:, :128] + both[:count, 128:]
    grad_hidden = grad_hidden + dot_nt(cot3[2 * PITCH : 2 * PITCH + count, :], rows[0])
    grad = grad_hidden * sigma * (1.0 + act * (1.0 - sigma))
    grad_act[...] = jnp.where(keep, grad, 0.0).astype(BF16)

    found = []
    for i in range(3):
        share = dot(flipped_cot, cells(hidden3, INNER[0] + PITCH * (i - 1) - HIDDEN[0]))
        share = (share * SCALE).astype(BF16)
        found += [share[:, j * 128 : j * 128 + 128] for j in range(3)]
    found.append(jnp.zeros((128, 128), BF16))
    for k in range(5):
        both = jnp.concatenate(found[2 * k : 2 * k + 2], axis=1)
        share_block(10 + k, dot_nt(pairs_t, both))
    flipped_grad = transposed(cells(grad_act, INNER[0] - begin))
    for i in range(3):
        share = dot(flipped_grad, cells(fine3, INNER[0] + PITCH * (i - 1)))
        share = (share * SCALE).astype(BF16)
        for j in range(3):
            share_block(3 * i + j, dot_nt(same, share[:, j * 256 : j * 256 + 256]))


def field_kernel(
    weights, second, fine, cot, hidden3, grad_act, down, result, coarse_gradient
):
    skip = first_block(weights, 9)
    begin, end = INNER
    total = dot(fine[...], skip)
    for i in range(3):
        kernels = jnp.concatenate([second[3 * i + j] for j in range(3)], axis=0)
        at = begin + PITCH * (i - 1) - HIDDEN[0]
        total = total + dot(hidden3[at : at + end - begin, :], kernels)
    total = total.astype(BF16)
    for r in range(8):
        result[r] = total[r * PITCH : r * PITCH + 64]

    grad3 = shifted(grad_act[...].astype(F32))
    begin, end = MIDDLE
    count = end - begin
    back = dot_nt(cot[...], skip)
    for i in range(3):
        kernels = jnp.concatenate([first_block(weights, 3 * i + 2 - j) for j in range(3)], axis=1)
        at = begin - PITCH * (i - 1) - WIDE[0]
        back = back + dot_nt(grad3[at : at + count], kernels)
    fine_gradient = jnp.where(inside(begin, (count, 256)), back, 0.0).astype(BF16)
    spread_t = permutation(256, spread_row, False)
    for j in range(4):
        part = dot(down[...], fine_gradient[2 * j * PITCH : 2 * j * PITCH + 4 * PITCH + 16])
        coarse_gradient[j] = dot(part.astype(BF16), spread_t).astype(BF16)


def call(kernel, outs, *operands, spaces="", scratch=(), semaphores=0, dtype=BF16, vmem=16):
    kinds = dict(h=pltpu.HBM, v=pltpu.VMEM)
    specs = [pl.BlockSpec(memory_space=kinds[k]) for k in spaces]
    return pl.pallas_call(
        kernel,
        out_shape=[jax.ShapeDtypeStruct(shape, dtype) for shape in outs],
        in_specs=specs[: len(operands)],
        out_specs=specs[len(operands) :],
        scratch_shapes=[pltpu.VMEM(*s) for s in scratch]
        + ([pltpu.SemaphoreType.DMA((semaphores,))] if semaphores else []),
        compiler_params=pltpu.CompilerParams(vmem_limit_bytes=vmem * 1024 * 1024),
    )(*operands)


def pairwise(first, second, axis, periodic):
    count = lax.axis_size(axis)
    ends = [(i, (i + 1) % count) for i in range(count if periodic else count - 1)]
    steps = [[(a, b), (b, a)] for a, b in ends]
    return (
        lax.ppermute(first, axis, [p for step in steps[0::2] for p in step]),
        lax.ppermute(second, axis, [p for step in steps[1::2] for p in step]),
    )


def on_device(coarse, w_first, w_second, w_skip, cotangent):
    up, down = jnp.asarray(upsampling_matrices(), BF16), jnp.asarray(decimation_matrix(), BF16)
    sent, *edges = call(
        front_kernel, [(16, 8, 128)] + [(5, 64, 128)] * 2,
        w_first, w_second.reshape(9, 128), w_skip, coarse, cotangent,
        spaces="hhhhhvvv", vmem=60,
        scratch=[((32, 128), F32), ((9, 2, 128), BF16), ((9, 128), BF16), ((2, 128), BF16)],
        semaphores=9,
    )
    came = lax.all_to_all(sent, "z", 0, 0, tiled=True)
    lat_a, lat_b = pairwise(*edges, LAT, False)
    (sent,) = call(spread_kernel, [(32, 128, 128)], came, spaces="vv")
    sent, lat_a, lat_b = lax.optimization_barrier((sent, lat_a, lat_b))
    weights = lax.all_to_all(sent, PLANE, 0, 0, tiled=True).reshape(8, 4, 4, 32, 128)
    edges = call(
        lon_edge_kernel, [(8, 16, 128)] * 2, coarse, cotangent, lat_a, lat_b,
        spaces="vvvvvv", scratch=[((5, 64, 128), BF16)] * 2,
    )
    lon_a, lon_b = pairwise(*edges, LON, True)
    blocks = (8, 4, 4, 32, 128)
    kept = [
        (10, 128, 128), (INNER[1] - INNER[0], 256), (MIDDLE[1] - MIDDLE[0], 128),
        (HIDDEN[1] - HIDDEN[0], 384), (WIDE[1] - WIDE[0], 128),
    ]
    shares, second, fine, cot_kept, hidden3, grad_act = call(
        main_kernel, [blocks] + kept,
        weights, coarse, cotangent, lat_a, lat_b, lon_a, lon_b, up,
        spaces="v" * 14,
        scratch=[
            (shape, BF16)
            for shape in [
                (5, 64, 128), (5, 64, 128), (8, 16, 128), (8, 16, 128), (LENGTH, 768), (LENGTH, 384), (480, 256),
            ]
        ]
        + [((LENGTH, 128), F32)],
    )
    came = lax.all_to_all(shares.reshape(32, 128, 128), PLANE, 0, 0, tiled=True)
    (sent,) = call(plane_sum_kernel, [(16, 2, 8, 128)], came, spaces="vv")
    came = lax.all_to_all(sent.reshape(32, 8, 128), ("z", "xl"), 0, 0, tiled=True)
    result, coarse_gradient = call(
        field_kernel, [(8, 64, 128), (4, 32, 256)],
        weights, second, fine, cot_kept, hidden3, grad_act, down,
        spaces="vvvvvvvvv",
    )
    came, result, coarse_gradient = lax.optimization_barrier((came, result, coarse_gradient))
    (mine,) = call(column_sum_kernel, [(2, 8, 128)], came.reshape(16, 2, 8, 128), spaces="vv", dtype=F32)
    other = lax.ppermute(mine, "core", [(0, 1), (1, 0)])
    grads = call(
        final_kernel, [(9, 2, 128), (9, 1, 128), (2, 128)],
        mine, other, spaces="vvvvv", dtype=F32,
    )
    return result, coarse_gradient, *grads


def solution(mesh):
    axes = ("xl", "core", "z", "xh", "y")
    fine = Mesh(mesh.devices.reshape(2, 2, 16, 2, 4), axes)
    field, taps, plain = P(LAT, LON, None), P(None, LON, None), P(LON, None)
    return jax.shard_map(
        on_device,
        mesh=fine,
        in_specs=(field, taps, taps, plain, field),
        out_specs=(field, field, taps, taps, plain),
        check_vma=False,
    )
```

```python
import jax
import jax.numpy as jnp
import numpy as np
from jax import lax
from jax.experimental import pallas as pl
from jax.experimental.pallas import tpu as pltpu
from jax.sharding import Mesh, PartitionSpec as P

PITCH = 80
LENGTH = 14 * PITCH + 16
WIDE = (PITCH, 12 * PITCH + 96)
MIDDLE = (2 * PITCH, 12 * PITCH + 16)
HIDDEN = (2 * PITCH + 16, 12 * PITCH)
INNER = (256, 880)
F32 = jnp.float32
BF16 = jnp.bfloat16
SCALE = 1.0 / 512.0
LAT = ("xl", "core")
LON = ("z", "xh", "y")
PLANE = ("xh", "y", "xl", "core")


def upsampling_matrices():
    taps = {}
    for parity in range(2):
        for dc in (-1, 0, 1):
            for u in range(PITCH):
                row, col = (parity - 1, 64 + u + dc) if u < 8 else (parity, u - 16 + dc)
                if not -3 <= col <= 66:
                    continue
                for wr, m in ((0.75, row // 2), (0.25, row // 2 + (1 if row % 2 else -1))):
                    for wc, n in ((0.75, col // 2), (0.25, col // 2 + (1 if col % 2 else -1))):
                        taps[parity, (dc + 1) * PITCH + u, (m + 1) * 48 + n % 48] = wr * wc
    out = np.zeros((2, 3 * PITCH, 144), np.float32)
    for place, weight in taps.items():
        out[place] = weight
    return out


def decimation_matrix():
    out = np.zeros((32, 4 * PITCH + 16), np.float32)
    weights = (0.25, 0.75, 0.75, 0.25)
    for j in range(32):
        for a in range(4):
            for b in range(4):
                out[j, a * PITCH + 16 + 2 * j - 1 + b] = weights[a] * weights[b]
    return out


def spread_row(column):
    return ((column >> 1) & 15) * 16 + (column >> 5) * 2 + (column & 1)


def pair_row(column):
    return (column & 1) * 128 + ((column >> 1) & 15) * 8 + (column >> 5)


def block_row(row):
    return ((row >> 1) & 15) * 8 + (row >> 5) * 2 + (row & 1)


def permutation(size, place, by_column):
    rows = lax.broadcasted_iota(jnp.int32, (size, size), 0)
    columns = lax.broadcasted_iota(jnp.int32, (size, size), 1)
    same = rows == place(columns) if by_column else columns == place(rows)
    return jnp.where(same, 1.0, 0.0).astype(BF16)


def lat_place():
    return lax.axis_index("xl") * 2 + lax.axis_index("core")


def in_odd_column():
    return lax.rem(lax.axis_index("y"), 2) == 1


def in_second_core():
    return lax.axis_index("core") == 1


def dot(a, b):
    return lax.dot_general(a, b, (((1,), (0,)), ((), ())), preferred_element_type=F32)


def dot_nt(a, b):
    return lax.dot_general(a, b, (((1,), (1,)), ((), ())), preferred_element_type=F32)


def inside(begin, shape):
    lat = lat_place()
    low, high = jnp.where(lat == 0, 248, 0), jnp.where(lat == 3, 888, LENGTH)
    place = lax.broadcasted_iota(jnp.int32, shape, 0) + begin
    return (place >= low) & (place < high)


def shifted(field):
    count = field.shape[0]
    return jnp.concatenate(
        [
            pltpu.roll(field, 1, 0).astype(BF16),
            field.astype(BF16),
            pltpu.roll(field, count - 1, 0).astype(BF16),
        ],
        axis=1,
    )


def cells(ref, begin, lanes=slice(None)):
    return jnp.concatenate(
        [ref[begin + PITCH * r : begin + PITCH * r + 64, lanes] for r in range(8)], axis=0
    )


def transposed(field):
    return field.astype(F32).T.astype(BF16)


def identity():
    return permutation(256, lambda row: row, True)


def copied(pairs, semaphores):
    copies = [pltpu.make_async_copy(a, b, semaphores.at[i]) for i, (a, b) in enumerate(pairs)]
    for copy in copies:
        copy.start()
    return copies


def finish(copies):
    for copy in copies:
        copy.wait()


def either(flag, a, b):
    return jnp.where(flag, a.astype(F32), b.astype(F32)).astype(BF16)


def exchanged(swap, moves, out_a, out_b, semaphores):
    @pl.when(swap)
    def _():
        finish(copied(moves(out_b, out_a), semaphores))

    @pl.when(jnp.logical_not(swap))
    def _():
        finish(copied(moves(out_a, out_b), semaphores))


def front_kernel(
    first, second, skip, coarse, cot, sent, out_a, out_b, rows, first_here, second_here, skip_here, semaphores
):
    def moves(up, down):
        found = []
        for out, r, m in ((up, 5, 2), (down, 0, 0)):
            found.append((cot.at[r : r + 3], out.at[0:3]))
            for h in range(2):
                lanes = slice(128 * h, 128 * h + 128)
                found.append((coarse.at[m : m + 2, :, lanes], out.at[3:5, 32 * h : 32 * h + 32]))
        return found

    copies = copied([(first, first_here), (second, second_here), (skip, skip_here)], semaphores.at[6:9])
    rows[...] = jnp.zeros((32, 128), F32)
    exchanged(in_second_core(), moves, out_a, out_b, semaphores)
    finish(copies)
    for k in range(9):
        rows[2 * k : 2 * k + 2] = first_here[k].astype(F32)
    rows[20:29] = second_here[...].astype(F32)
    rows[18:20] = skip_here[...].astype(F32)
    piece = rows[pl.ds(pl.multiple_of(lat_place() * 8, 8), 8)].astype(BF16)
    sent[...] = jnp.broadcast_to(piece[None], (16, 8, 128))


def edge_at(m, h):
    return 16 + 8 * h + m


def lon_edge_kernel(coarse, cot, lat_a, lat_b, out_a, out_b, low, high):
    odd = in_odd_column()
    sides(lat_a, lat_b, low, high, in_second_core())
    ups, downs = [jnp.zeros((4, 128), F32)] * 32, [jnp.zeros((4, 128), F32)] * 32
    for r in range(-3, 11):
        ref, k = cot_row(cot, low, high, r)
        ups[r + 3] = ref[k, 48:64].astype(F32)[12:]
        downs[r + 3] = ref[k, 0:16].astype(F32)[:4]
    for m in range(-2, 6):
        for h in range(2):
            row = coarse_row(coarse, low, high, m, h).astype(F32)
            ups[edge_at(m, h)] = row[28:32]
            downs[edge_at(m, h)] = row[0:4]
    for k in range(8):
        up = jnp.concatenate(ups[4 * k : 4 * k + 4], axis=0)
        down = jnp.concatenate(downs[4 * k : 4 * k + 4], axis=0)
        out_a[k] = either(odd, down, up)
        out_b[k] = either(odd, up, down)


def sides(first, second, low, high, swap):
    low[...] = either(swap, first[...], second[...])
    high[...] = either(swap, second[...], first[...])


def cot_row(cot, low, high, r):
    return (low, r + 3) if r < 0 else (cot, r) if r < 8 else (high, r - 8)


def coarse_row(coarse, low, high, m, h):
    if 0 <= m < 4:
        return coarse[m, :, 128 * h : 128 * h + 128]
    ref, k = (low, 5 + m) if m < 0 else (high, m - 1)
    return ref[k, 32 * h : 32 * h + 32]


def spread_kernel(came, sent, block, semaphores):
    order = permutation(128, block_row, False)
    block[...] = dot(order, came[...].reshape(128, 128)).astype(BF16)
    finish(copied([(block, sent.at[k]) for k in range(32)], semaphores))


def prepare(coarse, cot, low, high, left, right, up, fine3, cot3, grid, field):
    empty = jnp.zeros((4, 128), F32)

    def group(ref, e):
        return ref[e // 4].astype(F32)[4 * (e % 4) : 4 * (e % 4) + 4]

    grid[0:48] = jnp.zeros((48, 256), BF16)
    grid[432:480] = jnp.zeros((48, 256), BF16)
    for m in range(-2, 6):
        at = (m + 3) * 48
        for h in range(2):
            lanes = slice(128 * h, 128 * h + 128)
            middle, e = coarse_row(coarse, low, high, m, h), edge_at(m, h)
            grid[at : at + 32, lanes] = middle
            margin = jnp.concatenate([group(right, e), empty, empty, group(left, e)], axis=0)
            grid[at + 32 : at + 48, lanes] = margin.astype(BF16)
    after = empty
    for r in range(-3, 11):
        at = (r + 3) * PITCH
        ref, k = cot_row(cot, low, high, r)
        field[at : at + 16] = jnp.concatenate([after, empty, empty, group(left, r + 3)], axis=0)
        field[at + 16 : at + 80] = ref[k].astype(F32)
        after = group(right, r + 3)
    field[14 * PITCH :] = jnp.concatenate([after, empty, empty, empty], axis=0)
    cot3[...] = shifted(field[...])

    ordered = dot(grid[...], permutation(256, spread_row, True)).astype(BF16)
    for r in range(-3, 12):
        j, parity = divmod(r, 2)
        block = dot(up[parity], ordered[(j + 2) * 48 : (j + 2) * 48 + 144])
        begin = (r + 3) * PITCH
        rows = min(PITCH, LENGTH - begin)
        keep = inside(begin, (rows, 256))
        for k in range(3):
            part = block[k * PITCH : k * PITCH + rows]
            fine3[begin : begin + rows, k * 256 : k * 256 + 256] = jnp.where(keep, part, 0.0).astype(BF16)


def plane_sum_kernel(came, sent):
    total = came[0].astype(F32)
    for k in range(1, 32):
        total = total + came[k].astype(F32)
    order = permutation(128, block_row, True)
    block = dot(order, total.astype(BF16)).astype(BF16).reshape(16, 8, 128)
    for k in range(2):
        sent[:, k] = block


def column_sum_kernel(came, total):
    part = came[0].astype(F32)
    for k in range(1, 16):
        part = part + came[k].astype(F32)
    total[...] = part


def final_kernel(mine, other, first, second, skip):
    low = jnp.logical_not(in_second_core())
    pieces = []
    for k in range(2):
        pieces += [jnp.where(low, mine[k], other[k]), jnp.where(low, other[k], mine[k])]
    total = jnp.concatenate(pieces, axis=0)
    for k in range(9):
        first[k] = total[2 * k : 2 * k + 2]
        second[k] = total[20 + k : 21 + k]
    skip[...] = total[18:20]


def first_block(weights, k):
    return weights[:, k // 4, k % 4].reshape(256, 128)


def main_kernel(
    weights, coarse, cot, lat_a, lat_b, lon_a, lon_b, up,
    shares, second, fine, cot_kept, hidden3, grad_act,
    low, high, left, right, fine3, cot3, grid, field,
):
    def share_block(b, block):
        shares[:, b // 4, b % 4] = block.astype(BF16).reshape(8, 32, 128)

    pairs, pairs_t = permutation(256, pair_row, True), permutation(256, pair_row, False)
    same = identity()
    sides(lat_a, lat_b, low, high, in_second_core())
    sides(lon_a, lon_b, left, right, in_odd_column())
    prepare(coarse, cot, low, high, left, right, up, fine3, cot3, grid, field)
    fine[...] = fine3[INNER[0] : INNER[1], 256:512]
    cot_kept[...] = cot3[MIDDLE[0] : MIDDLE[1], 128:256]
    flipped_cot = transposed(cells(cot3, INNER[0], slice(128, 256)))
    share = (dot(flipped_cot, cells(fine3, INNER[0], slice(256, 512))) * SCALE).astype(BF16)
    share_block(9, dot_nt(same, share))
    share_block(15, jnp.zeros((256, 128), F32))
    for k in range(5):
        block = dot(pairs, first_block(weights, 10 + k)).astype(BF16)
        second[2 * k] = block[:128]
        second[2 * k + 1] = block[128:]
    begin, end = WIDE
    count = end - begin
    rows = [
        jnp.concatenate([first_block(weights, 3 * i + j) for j in range(3)], axis=0) for i in range(3)
    ]
    both = dot(fine3[0 : count + PITCH, :], jnp.concatenate(rows[:2], axis=1))
    act = both[:count, :128] + both[PITCH:, 128:]
    act = act + dot(fine3[2 * PITCH : 2 * PITCH + count, :], rows[2])
    keep = inside(begin, (count, 128))
    sigma = jax.nn.sigmoid(act)
    hidden = jnp.where(keep, act * sigma, 0.0)
    hidden3[...] = shifted(hidden)[HIDDEN[0] - begin : HIDDEN[1] - begin]
    rows = [jnp.concatenate([second[3 * i + 2 - j] for j in range(3)], axis=1) for i in range(3)]
    both = dot_nt(cot3[0 : count + PITCH, :], jnp.concatenate(rows[1:], axis=0))
    grad_hidden = both[PITCH:, :128] + both[:count, 128:]
    grad_hidden = grad_hidden + dot_nt(cot3[2 * PITCH : 2 * PITCH + count, :], rows[0])
    grad = grad_hidden * sigma * (1.0 + act * (1.0 - sigma))
    grad_act[...] = jnp.where(keep, grad, 0.0).astype(BF16)

    found = []
    for i in range(3):
        share = dot(flipped_cot, cells(hidden3, INNER[0] + PITCH * (i - 1) - HIDDEN[0]))
        share = (share * SCALE).astype(BF16)
        found += [share[:, j * 128 : j * 128 + 128] for j in range(3)]
    found.append(jnp.zeros((128, 128), BF16))
    for k in range(5):
        both = jnp.concatenate(found[2 * k : 2 * k + 2], axis=1)
        share_block(10 + k, dot_nt(pairs_t, both))
    flipped_grad = transposed(cells(grad_act, INNER[0] - begin))
    for i in range(3):
        share = dot(flipped_grad, cells(fine3, INNER[0] + PITCH * (i - 1)))
        share = (share * SCALE).astype(BF16)
        for j in range(3):
            share_block(3 * i + j, dot_nt(same, share[:, j * 256 : j * 256 + 256]))


def field_kernel(
    weights, second, fine, cot, hidden3, grad_act, down, result, coarse_gradient
):
    skip = first_block(weights, 9)
    begin, end = INNER
    total = dot(fine[...], skip)
    for i in range(3):
        kernels = jnp.concatenate([second[3 * i + j] for j in range(3)], axis=0)
        at = begin + PITCH * (i - 1) - HIDDEN[0]
        total = total + dot(hidden3[at : at + end - begin, :], kernels)
    total = total.astype(BF16)
    for r in range(8):
        result[r] = total[r * PITCH : r * PITCH + 64]

    grad3 = shifted(grad_act[...].astype(F32))
    begin, end = MIDDLE
    count = end - begin
    back = dot_nt(cot[...], skip)
    for i in range(3):
        kernels = jnp.concatenate([first_block(weights, 3 * i + 2 - j) for j in range(3)], axis=1)
        at = begin - PITCH * (i - 1) - WIDE[0]
        back = back + dot_nt(grad3[at : at + count], kernels)
    fine_gradient = jnp.where(inside(begin, (count, 256)), back, 0.0).astype(BF16)
    spread_t = permutation(256, spread_row, False)
    for j in range(4):
        part = dot(down[...], fine_gradient[2 * j * PITCH : 2 * j * PITCH + 4 * PITCH + 16])
        coarse_gradient[j] = dot(part.astype(BF16), spread_t).astype(BF16)


def call(kernel, outs, *operands, spaces="", scratch=(), semaphores=0, dtype=BF16, vmem=16):
    kinds = dict(h=pltpu.HBM, v=pltpu.VMEM)
    specs = [pl.BlockSpec(memory_space=kinds[k]) for k in spaces]
    return pl.pallas_call(
        kernel,
        out_shape=[jax.ShapeDtypeStruct(shape, dtype) for shape in outs],
        in_specs=specs[: len(operands)],
        out_specs=specs[len(operands) :],
        scratch_shapes=[pltpu.VMEM(*s) for s in scratch]
        + ([pltpu.SemaphoreType.DMA((semaphores,))] if semaphores else []),
        compiler_params=pltpu.CompilerParams(vmem_limit_bytes=vmem * 1024 * 1024),
    )(*operands)


def pairwise(first, second, axis, periodic):
    count = lax.axis_size(axis)
    ends = [(i, (i + 1) % count) for i in range(count if periodic else count - 1)]
    steps = [[(a, b), (b, a)] for a, b in ends]
    return (
        lax.ppermute(first, axis, [p for step in steps[0::2] for p in step]),
        lax.ppermute(second, axis, [p for step in steps[1::2] for p in step]),
    )


def on_device(coarse, w_first, w_second, w_skip, cotangent):
    up, down = jnp.asarray(upsampling_matrices(), BF16), jnp.asarray(decimation_matrix(), BF16)
    sent, *edges = call(
        front_kernel, [(16, 8, 128)] + [(5, 64, 128)] * 2,
        w_first, w_second.reshape(9, 128), w_skip, coarse, cotangent,
        spaces="hhhhhvvv", vmem=60,
        scratch=[((32, 128), F32), ((9, 2, 128), BF16), ((9, 128), BF16), ((2, 128), BF16)],
        semaphores=9,
    )
    came = lax.all_to_all(sent, "z", 0, 0, tiled=True)
    lat_a, lat_b = pairwise(*edges, LAT, False)
    (sent,) = call(
        spread_kernel, [(32, 128, 128)], came, spaces="vh", scratch=[((128, 128), BF16)], semaphores=32
    )
    sent, lat_a, lat_b = lax.optimization_barrier((sent, lat_a, lat_b))
    weights = lax.all_to_all(sent, PLANE, 0, 0, tiled=True).reshape(8, 4, 4, 32, 128)
    edges = call(
        lon_edge_kernel, [(8, 16, 128)] * 2, coarse, cotangent, lat_a, lat_b,
        spaces="vvvvvv", scratch=[((5, 64, 128), BF16)] * 2,
    )
    lon_a, lon_b = pairwise(*edges, LON, True)
    blocks = (8, 4, 4, 32, 128)
    kept = [
        (10, 128, 128), (INNER[1] - INNER[0], 256), (MIDDLE[1] - MIDDLE[0], 128),
        (HIDDEN[1] - HIDDEN[0], 384), (WIDE[1] - WIDE[0], 128),
    ]
    shares, second, fine, cot_kept, hidden3, grad_act = call(
        main_kernel, [blocks] + kept,
        weights, coarse, cotangent, lat_a, lat_b, lon_a, lon_b, up,
        spaces="v" * 14,
        scratch=[
            (shape, BF16)
            for shape in [
                (5, 64, 128), (5, 64, 128), (8, 16, 128), (8, 16, 128), (LENGTH, 768), (LENGTH, 384), (480, 256),
            ]
        ]
        + [((LENGTH, 128), F32)],
    )
    came = lax.all_to_all(shares.reshape(32, 128, 128), PLANE, 0, 0, tiled=True)
    (sent,) = call(plane_sum_kernel, [(16, 2, 8, 128)], came, spaces="vv")
    came = lax.all_to_all(sent.reshape(32, 8, 128), ("z", "xl"), 0, 0, tiled=True)
    result, coarse_gradient = call(
        field_kernel, [(8, 64, 128), (4, 32, 256)],
        weights, second, fine, cot_kept, hidden3, grad_act, down,
        spaces="vvvvvvvvv",
    )
    came, result, coarse_gradient = lax.optimization_barrier((came, result, coarse_gradient))
    (mine,) = call(column_sum_kernel, [(2, 8, 128)], came.reshape(16, 2, 8, 128), spaces="vv", dtype=F32)
    other = lax.ppermute(mine, "core", [(0, 1), (1, 0)])
    grads = call(
        final_kernel, [(9, 2, 128), (9, 1, 128), (2, 128)],
        mine, other, spaces="vvvvv", dtype=F32,
    )
    return result, coarse_gradient, *grads


def solution(mesh):
    axes = ("xl", "core", "z", "xh", "y")
    fine = Mesh(mesh.devices.reshape(2, 2, 16, 2, 4), axes)
    field, taps, plain = P(LAT, LON, None), P(None, LON, None), P(LON, None)
    return jax.shard_map(
        on_device,
        mesh=fine,
        in_specs=(field, taps, taps, plain, field),
        out_specs=(field, field, taps, taps, plain),
        check_vma=False,
    )
```
